512 devices in a mesh: wide: 32 (over z, core), narrow: 16 (over x, y).
Axes of the slice: x: 4, y: 4, z: 16, core: 2. Of those that a mesh axis runs over, the one named last changes fastest.
Arguments:
- coded: bfloat16 [1024, 98304], P('narrow', 'wide'), may hold values from -0.5 to 1.5
- exponents: int32 [32, 98304], P('narrow', 'wide'), may hold values from -2 to 2
- boot_counts: int32 [16, 98304], P(None, 'wide'), may hold values from 0 to 8
- tile_rows: int32 [32], replicated, may hold values from 0 to 31, each once
Outputs:
- owned: float32 [16, 1024, 1024], P(None, 'wide', 'narrow')
The draws below stay inside these ranges and needn't reach their ends.
Inputs may be any that keep to these rules, and one draw needn't show every extreme that they name: tile_rows holds each of 0 to 31 once.
All inputs are finite; a program needn't handle non-finite values.
Results may differ from the reference program's by a relative error of at most 0.0003.
Values may be sent and summed in bfloat16 or wider, within the bound.
A program may use at most 64 MiB of HBM per device.

```python
import jax
import jax.numpy as jnp
from jax import lax

F = 1024
R = 16
QB = 32
TOTAL = 98304
TILE = 32
N_WIDE = 32


def set_ends(entries, rng, least, top_value):
    extent = entries.shape
    spot = [jax.random.randint(jax.random.fold_in(rng, axis), (), 0, extent[axis]) for axis in range(len(extent))]
    entries = entries.at[tuple(spot)].set(least)
    longest = extent.index(max(extent))
    spot[longest] = (spot[longest] + 1) % extent[longest]
    return entries.at[tuple(spot)].set(top_value)


def shard_levels(stream_key, dims, pieces, low, high):
    def one(dim, blocks):
        draws = jax.random.uniform(jax.random.fold_in(jax.random.fold_in(stream_key, 6), dim), (blocks,), jnp.float32, low / len(pieces), high / len(pieces))
        return jnp.repeat(jnp.exp(draws), dims[dim] // blocks).reshape((-1,) + (1,) * (len(dims) - dim - 1))

    factor_of = one(*pieces[0])
    for cut in pieces[1:]:
        factor_of = factor_of * one(*cut)
    return factor_of


def setup_inputs(seed: int = 0) -> dict:
    seeds = jax.random.split(jax.random.key(seed), 5)
    coded = jnp.clip(-0.5 + 2.0 * jax.random.uniform(seeds[0], (F, TOTAL), jnp.float32) ** shard_levels(seeds[0], (F, TOTAL), ((0, 16), (1, 32)), -0.2, 0.2), -0.5, 1.5).astype(jnp.bfloat16)
    exponents = set_ends(jax.random.randint(seeds[1], (F // QB, TOTAL), -2, 3), jax.random.fold_in(seeds[1], 1), -2, 2).astype(jnp.int32)
    boot_counts = set_ends(jax.random.randint(seeds[2], (R, TOTAL), 0, 9), jax.random.fold_in(seeds[2], 1), 0, 8).astype(jnp.int32)
    tile_rows = jax.random.permutation(seeds[3], N_WIDE).astype(jnp.int32)
    return dict(coded=coded, exponents=exponents, boot_counts=boot_counts, tile_rows=tile_rows)


def reference(coded, exponents, boot_counts, tile_rows):
    scale = jnp.repeat(jnp.exp2(exponents.astype(jnp.float32)), QB, axis=0)
    features = (coded.astype(jnp.float32) * scale).astype(jnp.bfloat16).astype(jnp.float32)

    def one_replica(count_row):
        weighted = (features * count_row.astype(jnp.float32)[None, :]).astype(jnp.bfloat16)
        weighted = lax.optimization_barrier(weighted).astype(jnp.float32)
        gram = lax.dot_general(features, weighted, (((1,), (1,)), ((), ())),
                               precision=lax.Precision.HIGHEST,
                               preferred_element_type=jnp.float32)
        return jnp.tril(gram / TOTAL)

    grams = lax.map(one_replica, boot_counts)
    tiles = grams.reshape(R, N_WIDE, TILE, F)
    owned = jnp.take(tiles, tile_rows, axis=1)
    return owned.reshape(R, F, F)
```

```python
import jax
import jax.numpy as jnp
from jax import lax
from jax.experimental import pallas as pl
from jax.experimental.pallas import tpu as pltpu
from jax.sharding import PartitionSpec as P

MESH = pl.DeviceIdType.MESH
QB = 32
SIDE = 4
NZ = 16
WIDE = 32
COLS = 64
HALF = 32
REPLICAS = 16
TOTAL = 98304
CHUNKS = 4
F32 = jnp.float32
BF16 = jnp.bfloat16


def remote(src, dst, send_sem, recv_sem, wide, narrow):
    return pltpu.make_async_remote_copy(
        src_ref=src, dst_ref=dst, send_sem=send_sem, recv_sem=recv_sem,
        device_id={"wide": wide, "narrow": narrow}, device_id_type=MESH,
    )


def scale_exponent(largest):
    return jnp.ceil(jnp.log2(jnp.maximum(largest, 1e-30)))


def to_int16(values, factor):
    scaled = jnp.floor(values * factor + 0.5)
    return jnp.clip(scaled, -32767.0, 32767.0).astype(jnp.int32).astype(jnp.int16)


def from_int16(values, factor):
    return values.astype(jnp.int32).astype(F32) * factor


def put_coded(dst, index, parts):
    largest = jnp.max(jnp.abs(parts[0]), axis=0, keepdims=True)
    for part in parts[1:]:
        largest = jnp.maximum(largest, jnp.max(jnp.abs(part), axis=0, keepdims=True))
    exponent = scale_exponent(largest)
    factor = jnp.exp2(15.0 - exponent)
    for place, part in enumerate(parts):
        dst[(*index, pl.ds(64 * place, 64))] = to_int16(part, factor)
    tile = jnp.broadcast_to(exponent, (16, 128)).astype(jnp.int32).astype(jnp.int16)
    dst[(*index, pl.ds(64 * len(parts), 16))] = tile


def get_coded(src, index, place, count):
    tile = src[(*index, pl.ds(64 * count, 16))].astype(jnp.int32).astype(F32)
    factor = jnp.exp2(tile[0:1] - 15.0)
    return from_int16(src[(*index, pl.ds(64 * place, 64))], factor)


def kernel(coded, exponents, counts, tile_rows, out,
           xl, yl, cb, w1, w2, acc1, acc2, peer1, peer2, u, q1, near, far, u2, q2, last, f_buf,
           g_buf, r_buf, tiles, send_tiles, got,
           gs, gr, ps, pr, s1s, s1r, s2s, s2r, x1s, x1r, x2s, x2r):
    w = lax.axis_index("wide")
    n = lax.axis_index("narrow")
    z, c = w // 2, w % 2
    x, y = n // SIDE, n % SIDE
    k_all = coded.shape[1]
    kc_len = k_all // CHUNKS

    def at(x_, y_):
        return lax.rem(x_ + SIDE, SIDE) * SIDE + lax.rem(y_ + SIDE, SIDE)

    def zc(z_, c_):
        return lax.rem(z_ + NZ, NZ) * 2 + c_

    barrier = pltpu.get_barrier_semaphore()
    for d in range(1, SIDE):
        for narrow in (at(x + d, y), at(x, y + d)):
            pl.semaphore_signal(barrier, inc=1, device_id={"wide": w, "narrow": narrow}, device_id_type=MESH)

    def greet(d, carry):
        pl.semaphore_signal(barrier, inc=1, device_id={"wide": lax.rem(w + d, WIDE), "narrow": n}, device_id_type=MESH)
        return carry

    lax.fori_loop(1, WIDE, greet, 0)

    for kc in range(CHUNKS):
        cols = pl.ds(kc * kc_len, kc_len)
        for half in range(2):
            scale = jnp.exp2(exponents[half:half + 1, cols].astype(F32))
            rows = pl.ds(half * QB, QB)
            block = (coded[rows, cols].astype(F32) * scale).astype(BF16)
            xl[kc, y, rows, :] = block
            yl[kc, x, rows, :] = block
        for r in range(REPLICAS):
            row = counts[r:r + 1, cols].astype(F32)
            cb[kc, r] = jnp.broadcast_to(row, (16, kc_len)).astype(BF16)

    pl.semaphore_wait(barrier, 2 * (SIDE - 1) + WIDE - 1)

    def own_copies(kc):
        src = xl.at[kc, y]
        return [
            remote(src, xl.at[kc, y], gs.at[kc, 0], gr.at[kc, 0], w, at(x, y + 1)),
            remote(src, xl.at[kc, y], gs.at[kc, 1], gr.at[kc, 1], w, at(x, y - 1)),
            remote(src, yl.at[kc, x], gs.at[kc, 2], gr.at[kc, 2], w, at(x + 1, y)),
            remote(src, yl.at[kc, x], gs.at[kc, 3], gr.at[kc, 3], w, at(x - 1, y)),
        ]

    def wrap(v):
        return lax.rem(v + SIDE, SIDE)

    lo, hi = pl.ds(0, HALF), pl.ds(HALF, HALF)

    def forward_copies(kc):
        ym, yp, xm, xp = wrap(y - 1), wrap(y + 1), wrap(x - 1), wrap(x + 1)
        return [
            remote(xl.at[kc, ym, lo], xl.at[kc, ym, lo], gs.at[kc, 4], gr.at[kc, 4], w, at(x, y + 1)),
            remote(xl.at[kc, yp, hi], xl.at[kc, yp, hi], gs.at[kc, 5], gr.at[kc, 5], w, at(x, y - 1)),
            remote(yl.at[kc, xm, lo], yl.at[kc, xm, lo], gs.at[kc, 6], gr.at[kc, 6], w, at(x + 1, y)),
            remote(yl.at[kc, xp, hi], yl.at[kc, xp, hi], gs.at[kc, 7], gr.at[kc, 7], w, at(x - 1, y)),
        ]

    def wait_near(kc):
        places = [xl.at[kc, wrap(y - 1)], xl.at[kc, wrap(y + 1)], yl.at[kc, wrap(x - 1)], yl.at[kc, wrap(x + 1)]]
        for i, place in enumerate(places):
            remote(place, place, gs.at[kc, i], gr.at[kc, i], w, at(x, y + 1)).wait_recv()

    def wait_far(kc):
        yo, xo = wrap(y + 2), wrap(x + 2)
        places = [xl.at[kc, yo, lo], xl.at[kc, yo, hi], yl.at[kc, xo, lo], yl.at[kc, xo, hi]]
        for i, place in enumerate(places):
            remote(place, place, gs.at[kc, 4 + i], gr.at[kc, 4 + i], w, at(x, y + 1)).wait_recv()

    dims = (((1,), (1,)), ((), ()))

    def compute(kc):
        x_all = xl[kc].reshape(SIDE * COLS, kc_len)
        y_all = yl[kc].reshape(SIDE * COLS, kc_len)

        def first(rp, carry):
            for k in range(2):
                count = cb[kc, 2 * rp + k]
                for y1 in range(SIDE):
                    for part in range(2):
                        feats = xl[kc, y1, 16 * part:16 * part + 16, :]
                        w1[pl.ds(128 * k + HALF * y1 + 16 * part, 16), :] = feats * count
            res = lax.dot_general(y_all, w1[...], dims, preferred_element_type=F32)
            if kc == 0:
                acc1[rp] = res
            else:
                acc1[rp] += res
            return carry

        lax.fori_loop(0, REPLICAS // 2, first, 0)

        for x1 in range(SIDE):
            @pl.when(x1 <= x)
            def _():
                for r in range(REPLICAS):
                    count = cb[kc, r]
                    for part in range(2):
                        feats = yl[kc, x1, HALF + 16 * part:HALF + 16 * part + 16, :]
                        w2[pl.ds(HALF * r + 16 * part, 16), :] = feats * count
                res = lax.dot_general(w2[...], x_all, dims, preferred_element_type=F32)
                if kc == 0:
                    acc2[x1] = res
                else:
                    acc2[x1] += res

    for kc in range(min(2, CHUNKS)):
        for copy in own_copies(kc):
            copy.start()
    for kc in range(CHUNKS):
        wait_near(kc)
        for copy in forward_copies(kc):
            copy.start()
        if kc + 2 < CHUNKS:
            for copy in own_copies(kc + 2):
                copy.start()
        if kc >= 1:
            wait_far(kc - 1)
            compute(kc - 1)
    wait_far(CHUNKS - 1)
    compute(CHUNKS - 1)

    other = zc(z, 1 - c)

    def peer_copy(kind, s):
        if kind == 0:
            place = (slice(None), pl.ds(64 * s, 64))
            return remote(acc1.at[place], peer1.at[place], ps.at[s], pr.at[s], other, n)
        return remote(acc2.at[s], peer2.at[s], ps.at[s], pr.at[s], other, n)

    def used(kind, s):
        return (s >= x) if kind == 0 else (s <= x)

    for kind in range(2):
        for s in range(SIDE):
            @pl.when(jnp.logical_and(c == 1 - kind, used(kind, s)))
            def _():
                peer_copy(kind, s).start()

    for kind in range(2):
        for s in range(SIDE):
            @pl.when(jnp.logical_and(c == kind, used(kind, s)))
            def _():
                peer_copy(kind, s).wait_recv()
                for r in range(REPLICAS):
                    if kind == 0:
                        place = (r // 2, pl.ds(64 * s, 64), pl.ds(128 * (r % 2), 128))
                        u[s, r % 4, r // 4] = acc1[place] + peer1[place]
                    else:
                        for half in range(2):
                            place = (s, pl.ds(HALF * r, HALF), pl.ds(128 * half, 128))
                            u[s, r % 4, r // 4, 32 * half:32 * half + 32, :] = acc2[place] + peer2[place]

    def live(s):
        return jnp.logical_or(jnp.logical_and(c == 0, s >= x), jnp.logical_and(c == 1, s <= x))

    cls = lax.rem(z, 4)

    def klass(d):
        return lax.rem(cls + d + 4, 4)

    def near_copies(s):
        return [
            remote(q1.at[s, klass(1)], near.at[0, s], s1s.at[0, s], s1r.at[0, s], zc(z + 1, c), n),
            remote(q1.at[s, klass(-1)], near.at[1, s], s1s.at[1, s], s1r.at[1, s], zc(z - 1, c), n),
            remote(q1.at[s, klass(2), 0], far.at[0, s], s1s.at[2, s], s1r.at[2, s], zc(z + 2, c), n),
            remote(q1.at[s, klass(2), 1], far.at[1, s], s1s.at[3, s], s1r.at[3, s], zc(z - 2, c), n),
        ]

    for s in range(SIDE):
        @pl.when(live(s))
        def _():
            copies = near_copies(s)
            for d, parts in ((2, copies[2:]), (1, copies[:1]), (-1, copies[1:2])):
                for half in range(2):
                    put_coded(q1, (s, klass(d), half), [u[s, klass(d), 2 * half], u[s, klass(d), 2 * half + 1]])
                for copy in parts:
                    copy.start()

    step = z // 4

    def hop_copy(s, d):
        i = lax.rem(step + d, 4)
        return remote(q2.at[s, i], last.at[d - 1, s], s2s.at[d - 1, s], s2r.at[d - 1, s], zc(cls + 4 * i, c), n)

    for s in range(SIDE):
        @pl.when(live(s))
        def _():
            for copy in near_copies(s):
                copy.wait_recv()
            for half in range(2):
                for place in range(2):
                    i = 2 * half + place
                    u2[s, i] = (
                        (u[s, cls, i] + get_coded(near, (0, s, half), place, 2))
                        + (get_coded(near, (1, s, half), place, 2) + get_coded(far, (half, s), place, 2))
                    )
            for d in (2, 1, 3):
                i = lax.rem(step + d, 4)
                put_coded(q2, (s, i), [u2[s, i]])
                hop_copy(s, d).start()

    for s in range(SIDE):
        @pl.when(live(s))
        def _():
            total = u2[s, step]
            for d in (1, 2, 3):
                hop_copy(s, d).wait_recv()
                total = total + get_coded(last, (d - 1, s), 0, 1)
            f_buf[s] = total

        @pl.when(jnp.logical_not(live(s)))
        def _():
            f_buf[s] = jnp.zeros((64, 128), F32)

    @pl.when(c == 0)
    def _():
        for y1 in range(SIDE):
            g_buf[y1] = jnp.concatenate([f_buf[x1, :, HALF * y1:HALF * y1 + HALF] for x1 in range(SIDE)], axis=1)

    @pl.when(c == 1)
    def _():
        for x1 in range(SIDE):
            turned = [f_buf[x1, HALF * half:HALF * half + HALF, :].T for half in range(2)]
            g_buf[x1] = jnp.concatenate([turned[y1 // 2][64 * (y1 % 2):64 * (y1 % 2) + 64] for y1 in range(SIDE)], axis=1)

    place = jnp.where(c == 0, y, x)

    def line_copy(d):
        to = lax.rem(place + d, SIDE)
        narrow = jnp.where(c == 0, at(x, to), at(to, y))
        return remote(g_buf.at[to], r_buf.at[place], x1s.at[d - 1], x1r.at[d - 1], w, narrow)

    for d in (2, 1, 3):
        line_copy(d).start()
    r_buf[place] = g_buf[place]
    for d in range(1, SIDE):
        spot = r_buf.at[lax.rem(place - d + SIDE, SIDE)]
        remote(spot, spot, x1s.at[d - 1], x1r.at[d - 1], w, n).wait_recv()

    sub = lax.broadcasted_iota(jnp.int32, (8, 128), 0)
    lane = lax.broadcasted_iota(jnp.int32, (8, 128), 1)
    offset = sub + 8 * (lane // HALF) - lane % HALF - COLS * n - HALF * c
    for q in range(SIDE):
        for hh in range(2):
            groups = [r_buf[q, 32 * hh + 8 * k:32 * hh + 8 * k + 8, :] for k in range(4)]
            for g in range(SIDE):
                t = 2 * jnp.where(c == 0, SIDE * g + q, SIDE * q + g) + hh
                tile = jnp.concatenate([group[:, HALF * g:HALF * g + HALF] for group in groups], axis=1)
                tiles[t] = jnp.where(offset + 32 * t >= 0, tile / TOTAL, 0.0)

    def pick(j, carry):
        send_tiles[j] = tiles[tile_rows[j]]
        return carry

    lax.fori_loop(0, WIDE, pick, 0)

    def tile_copy(d):
        j = lax.rem(w + d, WIDE)
        return remote(send_tiles.at[j], got.at[w], x2s, x2r, j, n)

    def send_one(d, carry):
        tile_copy(d).start()
        return carry

    lax.fori_loop(1, WIDE, send_one, 0)
    got[w] = send_tiles[w]

    for kc in range(CHUNKS):
        for copy in own_copies(kc) + forward_copies(kc):
            copy.wait_send()
    for kind in range(2):
        for s in range(SIDE):
            @pl.when(jnp.logical_and(c == 1 - kind, used(kind, s)))
            def _():
                peer_copy(kind, s).wait_send()
    for s in range(SIDE):
        @pl.when(live(s))
        def _():
            for copy in near_copies(s):
                copy.wait_send()
            for d in (1, 2, 3):
                hop_copy(s, d).wait_send()
    for d in range(1, SIDE):
        line_copy(d).wait_send()

    most = pl.ds(0, WIDE - 1)
    every = remote(send_tiles.at[most], got.at[most], x2s, x2r, w, n)
    every.wait_recv()
    for r in range(REPLICAS):
        both = [got[2 * r], got[2 * r + 1]]
        for k in range(4):
            out[r, 8 * k:8 * k + 8, :] = jnp.concatenate(
                [part[:, HALF * k:HALF * k + HALF] for part in both], axis=1)
    every.wait_send()


def per_device(coded, exponents, boot_counts, tile_rows):
    k_all = coded.shape[1]
    kc_len = k_all // CHUNKS
    vmem = pl.BlockSpec(memory_space=pltpu.VMEM)
    dma = pltpu.SemaphoreType.DMA
    i16 = jnp.int16
    scratch = [
        pltpu.VMEM((CHUNKS, SIDE, COLS, kc_len), BF16),
        pltpu.VMEM((CHUNKS, SIDE, COLS, kc_len), BF16),
        pltpu.VMEM((CHUNKS, REPLICAS, 16, kc_len), BF16),
        pltpu.VMEM((256, kc_len), BF16),
        pltpu.VMEM((HALF * REPLICAS, kc_len), BF16),
        pltpu.VMEM((REPLICAS // 2, 256, 256), F32),
        pltpu.VMEM((SIDE, HALF * REPLICAS, 256), F32),
        pltpu.VMEM((REPLICAS // 2, 256, 256), F32),
        pltpu.VMEM((SIDE, HALF * REPLICAS, 256), F32),
        pltpu.VMEM((SIDE, 4, 4, 64, 128), F32),
        pltpu.VMEM((SIDE, 4, 2, 144, 128), i16),
        pltpu.VMEM((2, SIDE, 2, 144, 128), i16),
        pltpu.VMEM((2, SIDE, 144, 128), i16),
        pltpu.VMEM((SIDE, 4, 64, 128), F32),
        pltpu.VMEM((SIDE, 4, 80, 128), i16),
        pltpu.VMEM((3, SIDE, 80, 128), i16),
        pltpu.VMEM((SIDE, 64, 128), F32),
        pltpu.VMEM((SIDE, 64, 128), F32),
        pltpu.VMEM((SIDE, 64, 128), F32),
        pltpu.VMEM((WIDE, 8, 128), F32),
        pltpu.VMEM((WIDE, 8, 128), F32),
        pltpu.VMEM((WIDE, 8, 128), F32),
        dma((CHUNKS, 8)), dma((CHUNKS, 8)),
        dma((SIDE,)), dma((SIDE,)),
        dma((4, SIDE)), dma((4, SIDE)),
        dma((3, SIDE)), dma((3, SIDE)),
        dma((3,)), dma((3,)),
        dma, dma,
    ]
    return pl.pallas_call(
        kernel,
        out_shape=jax.ShapeDtypeStruct((REPLICAS, 32, COLS), F32),
        in_specs=[vmem, vmem, vmem, pl.BlockSpec(memory_space=pltpu.SMEM)],
        out_specs=vmem,
        scratch_shapes=scratch,
        compiler_params=pltpu.CompilerParams(
            collective_id=0, has_side_effects=True, vmem_limit_bytes=48 * 1024 * 1024),
        cost_estimate=pl.CostEstimate(flops=2 * 1024 * 1024 * k_all, bytes_accessed=2 * 1024 * 1024, transcendentals=0),
    )(coded, exponents, boot_counts, tile_rows)


def solution(mesh):
    placed = (P("narrow", "wide"), P("narrow", "wide"), P(None, "wide"), P())
    return jax.shard_map(
        per_device, mesh=mesh, in_specs=placed, out_specs=P(None, "wide", "narrow"), check_vma=False
    )
```

```python
import jax
import jax.numpy as jnp
from jax import lax
from jax.experimental import pallas as pl
from jax.experimental.pallas import tpu as pltpu
from jax.sharding import PartitionSpec as P

MESH = pl.DeviceIdType.MESH
QB = 32
SIDE = 4
NZ = 16
WIDE = 32
COLS = 64
HALF = 32
REPLICAS = 16
TOTAL = 98304
UNIT = 256
CHUNKS = ((0, 5), (5, 5), (10, 2))
F32 = jnp.float32
BF16 = jnp.bfloat16


def remote(src, dst, send_sem, recv_sem, wide, narrow):
    return pltpu.make_async_remote_copy(
        src_ref=src, dst_ref=dst, send_sem=send_sem, recv_sem=recv_sem,
        device_id={"wide": wide, "narrow": narrow}, device_id_type=MESH,
    )


def scale_exponent(largest):
    return jnp.ceil(jnp.log2(jnp.maximum(largest, 1e-30)))


def to_int16(values, factor):
    scaled = jnp.floor(values * factor + 0.5)
    return jnp.clip(scaled, -32767.0, 32767.0).astype(jnp.int32).astype(jnp.int16)


def from_int16(values, factor):
    return values.astype(jnp.int32).astype(F32) * factor


def put_coded(dst, index, parts):
    largest = jnp.max(jnp.abs(parts[0]), axis=0, keepdims=True)
    for part in parts[1:]:
        largest = jnp.maximum(largest, jnp.max(jnp.abs(part), axis=0, keepdims=True))
    exponent = scale_exponent(largest)
    factor = jnp.exp2(15.0 - exponent)
    for place, part in enumerate(parts):
        dst[(*index, pl.ds(64 * place, 64))] = to_int16(part, factor)
    tile = jnp.broadcast_to(exponent, (16, 128)).astype(jnp.int32).astype(jnp.int16)
    dst[(*index, pl.ds(64 * len(parts), 16))] = tile


def get_coded(src, index, place, count):
    tile = src[(*index, pl.ds(64 * count, 16))].astype(jnp.int32).astype(F32)
    factor = jnp.exp2(tile[0:1] - 15.0)
    return from_int16(src[(*index, pl.ds(64 * place, 64))], factor)


def kernel(coded_in, exponents_in, counts_in, tile_rows, out,
           coded, exponents, counts, xl, yl, cb, acc1, acc2, peer1, peer2, u, q1, near, far, u2, q2, last, f_buf,
           g_buf, r_buf, tiles, send_tiles, got,
           ins, gs, gr, ps, pr, s1s, s1r, s2s, s2r, x1s, x1r, x2s, x2r):
    w = lax.axis_index("wide")
    n = lax.axis_index("narrow")
    z, c = w // 2, w % 2
    x, y = n // SIDE, n % SIDE
    units = coded.shape[1] // UNIT

    def at(x_, y_):
        return lax.rem(x_ + SIDE, SIDE) * SIDE + lax.rem(y_ + SIDE, SIDE)

    def zc(z_, c_):
        return lax.rem(z_ + NZ, NZ) * 2 + c_

    inputs = [
        pltpu.make_async_copy(src, dst, ins.at[i])
        for i, (src, dst) in enumerate(((coded_in, coded), (exponents_in, exponents), (counts_in, counts)))
    ]
    for copy in inputs:
        copy.start()

    barrier = pltpu.get_barrier_semaphore()
    for narrow in (at(x + 1, y), at(x - 1, y), at(x, y + 1), at(x, y - 1)):
        pl.semaphore_signal(barrier, inc=1, device_id={"wide": w, "narrow": narrow}, device_id_type=MESH)
    for wide in (zc(z, 1 - c), zc(z + 1, c), zc(z - 1, c), zc(z + 2, c), zc(z - 2, c), zc(z + 8, c)):
        pl.semaphore_signal(barrier, inc=1, device_id={"wide": wide, "narrow": n}, device_id_type=MESH)

    for copy in inputs:
        copy.wait()
    for k in range(units):
        cols = pl.ds(k * UNIT, UNIT)
        for half in range(2):
            scale = jnp.exp2(exponents[half:half + 1, cols].astype(F32))
            rows = pl.ds(half * QB, QB)
            block = (coded[rows, cols].astype(F32) * scale).astype(BF16)
            xl[k, y, rows, :] = block
            yl[k, x, rows, :] = block
        for r in range(REPLICAS):
            row = counts[r:r + 1, cols].astype(F32)
            cb[k, r] = jnp.broadcast_to(row, (16, UNIT)).astype(BF16)

    pl.semaphore_wait(barrier, 10)

    spans = [pl.ds(*chunk) for chunk in CHUNKS]

    def own_copies(kc):
        src = xl.at[spans[kc], y]
        return [
            remote(src, xl.at[spans[kc], y], gs.at[kc, 0], gr.at[kc, 0], w, at(x, y + 1)),
            remote(src, xl.at[spans[kc], y], gs.at[kc, 1], gr.at[kc, 1], w, at(x, y - 1)),
            remote(src, yl.at[spans[kc], x], gs.at[kc, 2], gr.at[kc, 2], w, at(x + 1, y)),
            remote(src, yl.at[spans[kc], x], gs.at[kc, 3], gr.at[kc, 3], w, at(x - 1, y)),
        ]

    def wrap(v):
        return lax.rem(v + SIDE, SIDE)

    lo, hi = pl.ds(0, HALF), pl.ds(HALF, HALF)

    def forward_copies(kc):
        ym, yp, xm, xp = wrap(y - 1), wrap(y + 1), wrap(x - 1), wrap(x + 1)
        return [
            remote(xl.at[spans[kc], ym, lo], xl.at[spans[kc], ym, lo], gs.at[kc, 4], gr.at[kc, 4], w, at(x, y + 1)),
            remote(xl.at[spans[kc], yp, hi], xl.at[spans[kc], yp, hi], gs.at[kc, 5], gr.at[kc, 5], w, at(x, y - 1)),
            remote(yl.at[spans[kc], xm, lo], yl.at[spans[kc], xm, lo], gs.at[kc, 6], gr.at[kc, 6], w, at(x + 1, y)),
            remote(yl.at[spans[kc], xp, hi], yl.at[spans[kc], xp, hi], gs.at[kc, 7], gr.at[kc, 7], w, at(x - 1, y)),
        ]

    def wait_near(kc):
        places = [xl.at[spans[kc], wrap(y - 1)], xl.at[spans[kc], wrap(y + 1)], yl.at[spans[kc], wrap(x - 1)], yl.at[spans[kc], wrap(x + 1)]]
        for i, place in enumerate(places):
            remote(place, place, gs.at[kc, i], gr.at[kc, i], w, at(x, y + 1)).wait_recv()

    def wait_far(kc):
        yo, xo = wrap(y + 2), wrap(x + 2)
        places = [xl.at[spans[kc], yo, lo], xl.at[spans[kc], yo, hi], yl.at[spans[kc], xo, lo], yl.at[spans[kc], xo, hi]]
        for i, place in enumerate(places):
            remote(place, place, gs.at[kc, 4 + i], gr.at[kc, 4 + i], w, at(x, y + 1)).wait_recv()

    dims = (((1,), (1,)), ((), ()))

    def joined(pieces):
        return jnp.concatenate(pieces, axis=1)

    def parts_of(kc):
        start, count = CHUNKS[kc]
        return range(start, start + count)

    def first(kc):
        rows = joined([yl[k].reshape(SIDE * COLS, UNIT) for k in parts_of(kc)])
        feats = [xl[k, :, 0:HALF, :].reshape(8, 16, UNIT) for k in parts_of(kc)]
        for rp in range(REPLICAS // 2):
            cols = [
                joined([(f * cb[k, r][None]).reshape(128, UNIT) for f, k in zip(feats, parts_of(kc))])
                for r in (2 * rp, 2 * rp + 1)
            ]
            res = lax.dot_general(rows, jnp.concatenate(cols, axis=0), dims, preferred_element_type=F32)
            if kc == 0:
                acc1[rp] = res
            else:
                acc1[rp] += res

    def second(kc, x1):
        rows = joined([xl[k].reshape(SIDE * COLS, UNIT) for k in parts_of(kc)])
        cols = []
        for k in parts_of(kc):
            feats = yl[k, x1, HALF:COLS, :].reshape(1, 2, 16, UNIT)
            cols.append((feats * cb[k][:, None]).reshape(HALF * REPLICAS, UNIT))
        res = lax.dot_general(joined(cols), rows, dims, preferred_element_type=F32)
        if kc == 0:
            acc2[x1] = res
        else:
            acc2[x1] += res

    def second_all(kc, then=None):
        for x1 in range(SIDE):
            @pl.when(x1 <= x)
            def _():
                second(kc, x1)
                if then is not None:
                    then(x1)

    other = zc(z, 1 - c)

    def peer_copy(kind, s):
        if kind == 0:
            place = (slice(None), pl.ds(64 * s, 64))
            return remote(acc1.at[place], peer1.at[place], ps.at[s], pr.at[s], other, n)
        return remote(acc2.at[s], peer2.at[s], ps.at[s], pr.at[s], other, n)

    def used(kind, s):
        return (s >= x) if kind == 0 else (s <= x)

    def start_all(copies):
        for copy in copies:
            copy.start()

    start_all(own_copies(0))
    start_all(own_copies(1))
    wait_near(0)
    start_all(forward_copies(0))
    start_all(own_copies(2))
    wait_near(1)
    start_all(forward_copies(1))
    wait_far(0)
    first(0)
    wait_near(2)
    start_all(forward_copies(2))
    second_all(0)
    wait_far(1)
    first(1)
    second_all(1)
    wait_far(2)

    @pl.when(c == 1)
    def _():
        first(2)
        for s in range(SIDE):
            @pl.when(used(0, s))
            def _():
                peer_copy(0, s).start()

    def send_second(s):
        @pl.when(c == 0)
        def _():
            peer_copy(1, s).start()

    second_all(2, send_second)

    @pl.when(c == 0)
    def _():
        first(2)

    for kind in range(2):
        for s in range(SIDE):
            @pl.when(jnp.logical_and(c == kind, used(kind, s)))
            def _():
                peer_copy(kind, s).wait_recv()
                for r in range(REPLICAS):
                    if kind == 0:
                        place = (r // 2, pl.ds(64 * s, 64), pl.ds(128 * (r % 2), 128))
                        u[s, r % 4, r // 4] = acc1[place] + peer1[place]
                    else:
                        for half in range(2):
                            place = (s, pl.ds(HALF * r, HALF), pl.ds(128 * half, 128))
                            u[s, r % 4, r // 4, 32 * half:32 * half + 32, :] = acc2[place] + peer2[place]

    def live(s):
        return jnp.logical_or(jnp.logical_and(c == 0, s >= x), jnp.logical_and(c == 1, s <= x))

    cls = lax.rem(z, 4)

    def klass(d):
        return lax.rem(cls + d + 4, 4)

    def near_copies(s):
        return [
            remote(q1.at[s, klass(1)], near.at[0, s], s1s.at[0, s], s1r.at[0, s], zc(z + 1, c), n),
            remote(q1.at[s, klass(-1)], near.at[1, s], s1s.at[1, s], s1r.at[1, s], zc(z - 1, c), n),
            remote(q1.at[s, klass(2), 0], far.at[0, s], s1s.at[2, s], s1r.at[2, s], zc(z + 2, c), n),
            remote(q1.at[s, klass(2), 1], far.at[1, s], s1s.at[3, s], s1r.at[3, s], zc(z - 2, c), n),
        ]

    for s in range(SIDE):
        @pl.when(live(s))
        def _():
            copies = near_copies(s)
            for d, parts in ((2, copies[2:]), (1, copies[:1]), (-1, copies[1:2])):
                for half in range(2):
                    put_coded(q1, (s, klass(d), half), [u[s, klass(d), 2 * half], u[s, klass(d), 2 * half + 1]])
                for copy in parts:
                    copy.start()

    step = z // 4

    def hop_copy(s, d):
        i = lax.rem(step + d, 4)
        return remote(q2.at[s, i], last.at[d - 1, s], s2s.at[d - 1, s], s2r.at[d - 1, s], zc(cls + 4 * i, c), n)

    for s in range(SIDE):
        @pl.when(live(s))
        def _():
            for copy in near_copies(s):
                copy.wait_recv()
            for half in range(2):
                for place in range(2):
                    i = 2 * half + place
                    u2[s, i] = (
                        (u[s, cls, i] + get_coded(near, (0, s, half), place, 2))
                        + (get_coded(near, (1, s, half), place, 2) + get_coded(far, (half, s), place, 2))
                    )
            for d in (2, 1, 3):
                i = lax.rem(step + d, 4)
                put_coded(q2, (s, i), [u2[s, i]])
                hop_copy(s, d).start()

    for s in range(SIDE):
        @pl.when(live(s))
        def _():
            total = u2[s, step]
            for d in (1, 2, 3):
                hop_copy(s, d).wait_recv()
                total = total + get_coded(last, (d - 1, s), 0, 1)
            f_buf[s] = total

        @pl.when(jnp.logical_not(live(s)))
        def _():
            f_buf[s] = jnp.zeros((64, 128), F32)

    @pl.when(c == 0)
    def _():
        for y1 in range(SIDE):
            g_buf[y1] = jnp.concatenate([f_buf[x1, :, HALF * y1:HALF * y1 + HALF] for x1 in range(SIDE)], axis=1)

    @pl.when(c == 1)
    def _():
        for x1 in range(SIDE):
            turned = [f_buf[x1, HALF * half:HALF * half + HALF, :].T for half in range(2)]
            g_buf[x1] = jnp.concatenate([turned[y1 // 2][64 * (y1 % 2):64 * (y1 % 2) + 64] for y1 in range(SIDE)], axis=1)

    place = jnp.where(c == 0, y, x)

    def line_copy(d, core):
        to = lax.rem(place + d, SIDE)
        narrow = jnp.where(c == 0, at(x, to), at(to, y))
        sem = 2 * d + core
        return remote(g_buf.at[to], r_buf.at[c, place], x1s.at[sem], x1r.at[c, d], zc(z, core), narrow)

    for d in (2, 1, 3):
        for core in range(2):
            line_copy(d, core).start()
    for core in range(2):
        @pl.when(c != core)
        def _():
            line_copy(0, core).start()
    r_buf[c, place] = g_buf[place]
    for kind in range(2):
        here = y if kind == 0 else x
        for d in range(SIDE):
            def arrived():
                spot = r_buf.at[kind, lax.rem(here - d + SIDE, SIDE)]
                remote(spot, spot, x1s.at[0], x1r.at[kind, d], other, n).wait_recv()
            if d == 0:
                pl.when(c != kind)(arrived)
            else:
                arrived()

    sub = lax.broadcasted_iota(jnp.int32, (8, 128), 0)
    lane = lax.broadcasted_iota(jnp.int32, (8, 128), 1)
    for kind in range(2):
        offset = sub + 8 * (lane // HALF) - lane % HALF - COLS * n - HALF * kind
        for q in range(SIDE):
            for hh in range(2):
                groups = [r_buf[kind, q, 32 * hh + 8 * k:32 * hh + 8 * k + 8, :] for k in range(4)]
                for g in range(SIDE):
                    t = 2 * (SIDE * g + q if kind == 0 else SIDE * q + g) + hh
                    tile = jnp.concatenate([group[:, HALF * g:HALF * g + HALF] for group in groups], axis=1)
                    tiles[t, 8 * kind:8 * kind + 8, :] = jnp.where(offset + 32 * t >= 0, tile / TOTAL, 0.0)

    def tile_copy(d):
        to = lax.rem(z + d, NZ)
        return remote(send_tiles.at[to], got.at[z], x2s, x2r, zc(to, c), n)

    for d in (8, 7, 9, 6, 10, 5, 11, 4, 12, 3, 13, 2, 14, 1, 15):
        to = lax.rem(z + d, NZ)
        send_tiles[to] = tiles[tile_rows[2 * to + c]]
        tile_copy(d).start()
    got[z] = tiles[tile_rows[w]]

    for kc in range(len(CHUNKS)):
        for copy in own_copies(kc) + forward_copies(kc):
            copy.wait_send()
    for kind in range(2):
        for s in range(SIDE):
            @pl.when(jnp.logical_and(c == 1 - kind, used(kind, s)))
            def _():
                peer_copy(kind, s).wait_send()
    for s in range(SIDE):
        @pl.when(live(s))
        def _():
            for copy in near_copies(s):
                copy.wait_send()
            for d in (1, 2, 3):
                hop_copy(s, d).wait_send()
    for d in range(1, SIDE):
        for core in range(2):
            line_copy(d, core).wait_send()
    for core in range(2):
        @pl.when(c != core)
        def _():
            line_copy(0, core).wait_send()

    most = pl.ds(0, NZ - 1)
    every = remote(send_tiles.at[most], got.at[most], x2s, x2r, other, n)
    every.wait_recv()
    for r in range(REPLICAS):
        for k in range(4):
            out[r, 8 * k:8 * k + 8, :] = jnp.concatenate(
                [got[r, 8 * kind:8 * kind + 8, HALF * k:HALF * k + HALF] for kind in range(2)], axis=1)
    every.wait_send()


def per_device(coded, exponents, boot_counts, tile_rows):
    k_all = coded.shape[1]
    units = k_all // UNIT
    vmem, hbm = pl.BlockSpec(memory_space=pltpu.VMEM), pl.BlockSpec(memory_space=pl.ANY)
    dma = pltpu.SemaphoreType.DMA
    i16 = jnp.int16
    scratch = [
        pltpu.VMEM(coded.shape, BF16),
        pltpu.VMEM(exponents.shape, jnp.int32),
        pltpu.VMEM(boot_counts.shape, jnp.int32),
        pltpu.VMEM((units, SIDE, COLS, UNIT), BF16),
        pltpu.VMEM((units, SIDE, COLS, UNIT), BF16),
        pltpu.VMEM((units, REPLICAS, 16, UNIT), BF16),
        pltpu.VMEM((REPLICAS // 2, 256, 256), F32),
        pltpu.VMEM((SIDE, HALF * REPLICAS, 256), F32),
        pltpu.VMEM((REPLICAS // 2, 256, 256), F32),
        pltpu.VMEM((SIDE, HALF * REPLICAS, 256), F32),
        pltpu.VMEM((SIDE, 4, 4, 64, 128), F32),
        pltpu.VMEM((SIDE, 4, 2, 144, 128), i16),
        pltpu.VMEM((2, SIDE, 2, 144, 128), i16),
        pltpu.VMEM((2, SIDE, 144, 128), i16),
        pltpu.VMEM((SIDE, 4, 64, 128), F32),
        pltpu.VMEM((SIDE, 4, 80, 128), i16),
        pltpu.VMEM((3, SIDE, 80, 128), i16),
        pltpu.VMEM((SIDE, 64, 128), F32),
        pltpu.VMEM((SIDE, 64, 128), F32),
        pltpu.VMEM((2, SIDE, 64, 128), F32),
        pltpu.VMEM((WIDE, 16, 128), F32),
        pltpu.VMEM((NZ, 16, 128), F32),
        pltpu.VMEM((NZ, 16, 128), F32),
        dma((3,)),
        dma((len(CHUNKS), 8)), dma((len(CHUNKS), 8)),
        dma((SIDE,)), dma((SIDE,)),
        dma((4, SIDE)), dma((4, SIDE)),
        dma((3, SIDE)), dma((3, SIDE)),
        dma((2 * SIDE,)), dma((2, SIDE)),
        dma, dma,
    ]
    return pl.pallas_call(
        kernel,
        out_shape=jax.ShapeDtypeStruct((REPLICAS, 32, COLS), F32),
        in_specs=[hbm, hbm, hbm, pl.BlockSpec(memory_space=pltpu.SMEM)],
        out_specs=vmem,
        scratch_shapes=scratch,
        compiler_params=pltpu.CompilerParams(
            collective_id=0, has_side_effects=True, vmem_limit_bytes=62 * 1024 * 1024),
        cost_estimate=pl.CostEstimate(flops=2 * 1024 * 1024 * k_all, bytes_accessed=2 * 1024 * 1024, transcendentals=0),
    )(coded, exponents, boot_counts, tile_rows)


def solution(mesh):
    placed = (P("narrow", "wide"), P("narrow", "wide"), P(None, "wide"), P())
    return jax.shard_map(
        per_device, mesh=mesh, in_specs=placed, out_specs=P(None, "wide", "narrow"), check_vma=False
    )
```

```python
import jax
import jax.numpy as jnp
from jax import lax
from jax.experimental import pallas as pl
from jax.experimental.pallas import tpu as pltpu
from jax.sharding import PartitionSpec as P

MESH = pl.DeviceIdType.MESH
QB = 32
SIDE = 4
NZ = 16
WIDE = 32
COLS = 64
HALF = 32
REPLICAS = 16
TOTAL = 98304
UNIT = 256
CHUNKS = ((0, 5), (5, 5), (10, 2))
F32 = jnp.float32
BF16 = jnp.bfloat16


def remote(src, dst, send_sem, recv_sem, wide, narrow):
    return pltpu.make_async_remote_copy(
        src_ref=src, dst_ref=dst, send_sem=send_sem, recv_sem=recv_sem,
        device_id={"wide": wide, "narrow": narrow}, device_id_type=MESH,
    )


def scale_exponent(largest):
    return jnp.ceil(jnp.log2(jnp.maximum(largest, 1e-30)))


def to_int16(values, factor):
    scaled = jnp.floor(values * factor + 0.5)
    return jnp.clip(scaled, -32767.0, 32767.0).astype(jnp.int32).astype(jnp.int16)


def from_int16(values, factor):
    return values.astype(jnp.int32).astype(F32) * factor


def put_coded(dst, index, parts):
    largest = jnp.max(jnp.abs(parts[0]), axis=0, keepdims=True)
    for part in parts[1:]:
        largest = jnp.maximum(largest, jnp.max(jnp.abs(part), axis=0, keepdims=True))
    exponent = scale_exponent(largest)
    factor = jnp.exp2(15.0 - exponent)
    for place, part in enumerate(parts):
        dst[(*index, pl.ds(64 * place, 64))] = to_int16(part, factor)
    tile = jnp.broadcast_to(exponent, (16, 128)).astype(jnp.int32).astype(jnp.int16)
    dst[(*index, pl.ds(64 * len(parts), 16))] = tile


def get_coded(src, index, place, count):
    tile = src[(*index, pl.ds(64 * count, 16))].astype(jnp.int32).astype(F32)
    factor = jnp.exp2(tile[0:1] - 15.0)
    return from_int16(src[(*index, pl.ds(64 * place, 64))], factor)


def kernel(coded_in, exponents_in, counts_in, tile_rows, out,
           coded, exponents, counts, xl, yl, cb, acc1, acc2, peer1, peer2, u, q1, near, far, u2, q2, last, f_buf,
           g_buf, r_buf, tiles, send_tiles, got,
           known1, known2, known4, ins, gs, gr, ps, pr, s1s, s1r, s2s, s2r, x1s, x1r, x2s, x2r):
    w = lax.axis_index("wide")
    n = lax.axis_index("narrow")
    z, c = w // 2, w % 2
    x, y = n // SIDE, n % SIDE
    units = coded.shape[1] // UNIT

    def at(x_, y_):
        return lax.rem(x_ + SIDE, SIDE) * SIDE + lax.rem(y_ + SIDE, SIDE)

    def zc(z_, c_):
        return lax.rem(z_ + NZ, NZ) * 2 + c_

    inputs = [
        pltpu.make_async_copy(src, dst, ins.at[i])
        for i, (src, dst) in enumerate(((coded_in, coded), (exponents_in, exponents), (counts_in, counts)))
    ]
    barrier = pltpu.get_barrier_semaphore()
    for narrow in (at(x + 1, y), at(x - 1, y), at(x, y + 1), at(x, y - 1)):
        pl.semaphore_signal(barrier, inc=1, device_id={"wide": w, "narrow": narrow}, device_id_type=MESH)
    for wide in (zc(z, 1 - c), zc(z + 1, c), zc(z - 1, c)):
        pl.semaphore_signal(barrier, inc=1, device_id={"wide": wide, "narrow": n}, device_id_type=MESH)

    for copy in inputs:
        copy.start()
    for copy in inputs[:2]:
        copy.wait()
    for k in range(units):
        cols = pl.ds(k * UNIT, UNIT)
        for half in range(2):
            scale = jnp.exp2(exponents[half:half + 1, cols].astype(F32))
            rows = pl.ds(half * QB, QB)
            block = (coded[rows, cols].astype(F32) * scale).astype(BF16)
            xl[k, y, rows, :] = block
            yl[k, x, rows, :] = block

    pl.semaphore_wait(barrier, 7)

    def tell(sem, d):
        for wide in (zc(z + d, c), zc(z - d, c)):
            pl.semaphore_signal(sem, inc=1, device_id={"wide": wide, "narrow": n}, device_id_type=MESH)

    spans = [pl.ds(*chunk) for chunk in CHUNKS]

    def own_copies(kc):
        src = xl.at[spans[kc], y]
        return [
            remote(src, xl.at[spans[kc], y], gs.at[kc, 0], gr.at[kc, 0], w, at(x, y + 1)),
            remote(src, xl.at[spans[kc], y], gs.at[kc, 1], gr.at[kc, 1], w, at(x, y - 1)),
            remote(src, yl.at[spans[kc], x], gs.at[kc, 2], gr.at[kc, 2], w, at(x + 1, y)),
            remote(src, yl.at[spans[kc], x], gs.at[kc, 3], gr.at[kc, 3], w, at(x - 1, y)),
        ]

    def wrap(v):
        return lax.rem(v + SIDE, SIDE)

    lo, hi = pl.ds(0, HALF), pl.ds(HALF, HALF)

    def forward_copies(kc):
        ym, yp, xm, xp = wrap(y - 1), wrap(y + 1), wrap(x - 1), wrap(x + 1)
        return [
            remote(xl.at[spans[kc], ym, lo], xl.at[spans[kc], ym, lo], gs.at[kc, 4], gr.at[kc, 4], w, at(x, y + 1)),
            remote(xl.at[spans[kc], yp, hi], xl.at[spans[kc], yp, hi], gs.at[kc, 5], gr.at[kc, 5], w, at(x, y - 1)),
            remote(yl.at[spans[kc], xm, lo], yl.at[spans[kc], xm, lo], gs.at[kc, 6], gr.at[kc, 6], w, at(x + 1, y)),
            remote(yl.at[spans[kc], xp, hi], yl.at[spans[kc], xp, hi], gs.at[kc, 7], gr.at[kc, 7], w, at(x - 1, y)),
        ]

    def wait_near(kc):
        places = [xl.at[spans[kc], wrap(y - 1)], xl.at[spans[kc], wrap(y + 1)], yl.at[spans[kc], wrap(x - 1)], yl.at[spans[kc], wrap(x + 1)]]
        for i, place in enumerate(places):
            remote(place, place, gs.at[kc, i], gr.at[kc, i], w, at(x, y + 1)).wait_recv()

    def wait_far(kc):
        yo, xo = wrap(y + 2), wrap(x + 2)
        places = [xl.at[spans[kc], yo, lo], xl.at[spans[kc], yo, hi], yl.at[spans[kc], xo, lo], yl.at[spans[kc], xo, hi]]
        for i, place in enumerate(places):
            remote(place, place, gs.at[kc, 4 + i], gr.at[kc, 4 + i], w, at(x, y + 1)).wait_recv()

    dims = (((1,), (1,)), ((), ()))

    def joined(pieces):
        return jnp.concatenate(pieces, axis=1)

    def parts_of(kc):
        start, count = CHUNKS[kc]
        return range(start, start + count)

    def first(kc):
        rows = joined([yl[k].reshape(SIDE * COLS, UNIT) for k in parts_of(kc)])
        feats = [xl[k, :, 0:HALF, :].reshape(8, 16, UNIT) for k in parts_of(kc)]
        for rp in range(REPLICAS // 2):
            cols = [
                joined([(f * cb[k, r][None]).reshape(128, UNIT) for f, k in zip(feats, parts_of(kc))])
                for r in (2 * rp, 2 * rp + 1)
            ]
            res = lax.dot_general(rows, jnp.concatenate(cols, axis=0), dims, preferred_element_type=F32)
            if kc == 0:
                acc1[rp] = res
            else:
                acc1[rp] += res

    def second(kc, x1):
        rows = joined([xl[k].reshape(SIDE * COLS, UNIT) for k in parts_of(kc)])
        cols = []
        for k in parts_of(kc):
            feats = yl[k, x1, HALF:COLS, :].reshape(1, 2, 16, UNIT)
            cols.append((feats * cb[k][:, None]).reshape(HALF * REPLICAS, UNIT))
        res = lax.dot_general(joined(cols), rows, dims, preferred_element_type=F32)
        if kc == 0:
            acc2[x1] = res
        else:
            acc2[x1] += res

    def second_all(kc, then=None):
        for x1 in range(SIDE):
            @pl.when(x1 <= x)
            def _():
                second(kc, x1)
                if then is not None:
                    then(x1)

    other = zc(z, 1 - c)

    def peer_copy(kind, s):
        if kind == 0:
            place = (slice(None), pl.ds(64 * s, 64))
            return remote(acc1.at[place], peer1.at[place], ps.at[s], pr.at[s], other, n)
        return remote(acc2.at[s], peer2.at[s], ps.at[s], pr.at[s], other, n)

    def used(kind, s):
        return (s >= x) if kind == 0 else (s <= x)

    def start_all(copies):
        for copy in copies:
            copy.start()

    start_all(own_copies(0))
    start_all(own_copies(1))
    tell(known1, 1)
    inputs[2].wait()
    for k in range(units):
        for r in range(REPLICAS):
            row = counts[r:r + 1, k * UNIT:(k + 1) * UNIT].astype(F32)
            cb[k, r] = jnp.broadcast_to(row, (16, UNIT)).astype(BF16)
    wait_near(0)
    start_all(forward_copies(0))
    start_all(own_copies(2))
    pl.semaphore_wait(known1, 2)
    tell(known2, 2)
    wait_near(1)
    start_all(forward_copies(1))
    pl.semaphore_wait(known2, 2)
    tell(known4, 4)
    wait_far(0)
    first(0)
    wait_near(2)
    start_all(forward_copies(2))
    pl.semaphore_wait(known4, 2)
    second_all(0)
    wait_far(1)
    first(1)
    second_all(1)
    wait_far(2)

    @pl.when(c == 1)
    def _():
        first(2)
        for s in range(SIDE):
            @pl.when(used(0, s))
            def _():
                peer_copy(0, s).start()

    def send_second(s):
        @pl.when(c == 0)
        def _():
            peer_copy(1, s).start()

    second_all(2, send_second)

    @pl.when(c == 0)
    def _():
        first(2)

    for kind in range(2):
        for s in range(SIDE):
            @pl.when(jnp.logical_and(c == kind, used(kind, s)))
            def _():
                peer_copy(kind, s).wait_recv()
                for r in range(REPLICAS):
                    if kind == 0:
                        place = (r // 2, pl.ds(64 * s, 64), pl.ds(128 * (r % 2), 128))
                        u[s, r % 4, r // 4] = acc1[place] + peer1[place]
                    else:
                        for half in range(2):
                            place = (s, pl.ds(HALF * r, HALF), pl.ds(128 * half, 128))
                            u[s, r % 4, r // 4, 32 * half:32 * half + 32, :] = acc2[place] + peer2[place]

    def live(s):
        return jnp.logical_or(jnp.logical_and(c == 0, s >= x), jnp.logical_and(c == 1, s <= x))

    cls = lax.rem(z, 4)

    def klass(d):
        return lax.rem(cls + d + 4, 4)

    def near_copies(s):
        return [
            remote(q1.at[s, klass(1)], near.at[0, s], s1s.at[0, s], s1r.at[0, s], zc(z + 1, c), n),
            remote(q1.at[s, klass(-1)], near.at[1, s], s1s.at[1, s], s1r.at[1, s], zc(z - 1, c), n),
            remote(q1.at[s, klass(2), 0], far.at[0, s], s1s.at[2, s], s1r.at[2, s], zc(z + 2, c), n),
            remote(q1.at[s, klass(2), 1], far.at[1, s], s1s.at[3, s], s1r.at[3, s], zc(z - 2, c), n),
        ]

    for s in range(SIDE):
        @pl.when(live(s))
        def _():
            copies = near_copies(s)
            for d, parts in ((2, copies[2:]), (1, copies[:1]), (-1, copies[1:2])):
                for half in range(2):
                    put_coded(q1, (s, klass(d), half), [u[s, klass(d), 2 * half], u[s, klass(d), 2 * half + 1]])
                for copy in parts:
                    copy.start()

    step = z // 4

    def hop_copy(s, d):
        i = lax.rem(step + d, 4)
        return remote(q2.at[s, i], last.at[d - 1, s], s2s.at[d - 1, s], s2r.at[d - 1, s], zc(cls + 4 * i, c), n)

    for s in range(SIDE):
        @pl.when(live(s))
        def _():
            for copy in near_copies(s):
                copy.wait_recv()
            for half in range(2):
                for place in range(2):
                    i = 2 * half + place
                    u2[s, i] = (
                        (u[s, cls, i] + get_coded(near, (0, s, half), place, 2))
                        + (get_coded(near, (1, s, half), place, 2) + get_coded(far, (half, s), place, 2))
                    )
            for d in (2, 1, 3):
                i = lax.rem(step + d, 4)
                put_coded(q2, (s, i), [u2[s, i]])
                hop_copy(s, d).start()

    for s in range(SIDE):
        @pl.when(live(s))
        def _():
            total = u2[s, step]
            for d in (1, 2, 3):
                hop_copy(s, d).wait_recv()
                total = total + get_coded(last, (d - 1, s), 0, 1)
            f_buf[s] = total

        @pl.when(jnp.logical_not(live(s)))
        def _():
            f_buf[s] = jnp.zeros((64, 128), F32)

    @pl.when(c == 0)
    def _():
        for y1 in range(SIDE):
            g_buf[y1] = jnp.concatenate([f_buf[x1, :, HALF * y1:HALF * y1 + HALF] for x1 in range(SIDE)], axis=1)

    @pl.when(c == 1)
    def _():
        for x1 in range(SIDE):
            turned = [f_buf[x1, HALF * half:HALF * half + HALF, :].T for half in range(2)]
            g_buf[x1] = jnp.concatenate([turned[y1 // 2][64 * (y1 % 2):64 * (y1 % 2) + 64] for y1 in range(SIDE)], axis=1)

    place = jnp.where(c == 0, y, x)

    def line_copy(d, core):
        to = lax.rem(place + d, SIDE)
        narrow = jnp.where(c == 0, at(x, to), at(to, y))
        sem = 2 * d + core
        return remote(g_buf.at[to], r_buf.at[c, place], x1s.at[sem], x1r.at[c, d], zc(z, core), narrow)

    for d in (2, 1, 3):
        for core in range(2):
            line_copy(d, core).start()
    for core in range(2):
        @pl.when(c != core)
        def _():
            line_copy(0, core).start()
    r_buf[c, place] = g_buf[place]
    for kind in range(2):
        here = y if kind == 0 else x
        for d in range(SIDE):
            def arrived():
                spot = r_buf.at[kind, lax.rem(here - d + SIDE, SIDE)]
                remote(spot, spot, x1s.at[0], x1r.at[kind, d], other, n).wait_recv()
            if d == 0:
                pl.when(c != kind)(arrived)
            else:
                arrived()

    sub = lax.broadcasted_iota(jnp.int32, (8, 128), 0)
    lane = lax.broadcasted_iota(jnp.int32, (8, 128), 1)
    for kind in range(2):
        offset = sub + 8 * (lane // HALF) - lane % HALF - COLS * n - HALF * kind
        for q in range(SIDE):
            for hh in range(2):
                groups = [r_buf[kind, q, 32 * hh + 8 * k:32 * hh + 8 * k + 8, :] for k in range(4)]
                for g in range(SIDE):
                    t = 2 * (SIDE * g + q if kind == 0 else SIDE * q + g) + hh
                    tile = jnp.concatenate([group[:, HALF * g:HALF * g + HALF] for group in groups], axis=1)
                    tiles[t, 8 * kind:8 * kind + 8, :] = jnp.where(offset + 32 * t >= 0, tile / TOTAL, 0.0)

    def tile_copy(d):
        to = lax.rem(z + d, NZ)
        return remote(send_tiles.at[to], got.at[z], x2s, x2r, zc(to, c), n)

    for d in (8, 7, 9, 6, 10, 5, 11, 4, 12, 3, 13, 2, 14, 1, 15):
        to = lax.rem(z + d, NZ)
        send_tiles[to] = tiles[tile_rows[2 * to + c]]
        tile_copy(d).start()
    got[z] = tiles[tile_rows[w]]

    for kc in range(len(CHUNKS)):
        for copy in own_copies(kc) + forward_copies(kc):
            copy.wait_send()
    for kind in range(2):
        for s in range(SIDE):
            @pl.when(jnp.logical_and(c == 1 - kind, used(kind, s)))
            def _():
                peer_copy(kind, s).wait_send()
    for s in range(SIDE):
        @pl.when(live(s))
        def _():
            for copy in near_copies(s):
                copy.wait_send()
            for d in (1, 2, 3):
                hop_copy(s, d).wait_send()
    for d in range(1, SIDE):
        for core in range(2):
            line_copy(d, core).wait_send()
    for core in range(2):
        @pl.when(c != core)
        def _():
            line_copy(0, core).wait_send()

    most = pl.ds(0, NZ - 1)
    every = remote(send_tiles.at[most], got.at[most], x2s, x2r, other, n)
    every.wait_recv()
    for r in range(REPLICAS):
        for k in range(4):
            out[r, 8 * k:8 * k + 8, :] = jnp.concatenate(
                [got[r, 8 * kind:8 * kind + 8, HALF * k:HALF * k + HALF] for kind in range(2)], axis=1)
    every.wait_send()


def per_device(coded, exponents, boot_counts, tile_rows):
    k_all = coded.shape[1]
    units = k_all // UNIT
    vmem, hbm = pl.BlockSpec(memory_space=pltpu.VMEM), pl.BlockSpec(memory_space=pltpu.HBM)
    dma = pltpu.SemaphoreType.DMA
    i16 = jnp.int16
    scratch = [
        pltpu.VMEM(coded.shape, BF16),
        pltpu.VMEM(exponents.shape, jnp.int32),
        pltpu.VMEM(boot_counts.shape, jnp.int32),
        pltpu.VMEM((units, SIDE, COLS, UNIT), BF16),
        pltpu.VMEM((units, SIDE, COLS, UNIT), BF16),
        pltpu.VMEM((units, REPLICAS, 16, UNIT), BF16),
        pltpu.VMEM((REPLICAS // 2, 256, 256), F32),
        pltpu.VMEM((SIDE, HALF * REPLICAS, 256), F32),
        pltpu.VMEM((REPLICAS // 2, 256, 256), F32),
        pltpu.VMEM((SIDE, HALF * REPLICAS, 256), F32),
        pltpu.VMEM((SIDE, 4, 4, 64, 128), F32),
        pltpu.VMEM((SIDE, 4, 2, 144, 128), i16),
        pltpu.VMEM((2, SIDE, 2, 144, 128), i16),
        pltpu.VMEM((2, SIDE, 144, 128), i16),
        pltpu.VMEM((SIDE, 4, 64, 128), F32),
        pltpu.VMEM((SIDE, 4, 80, 128), i16),
        pltpu.VMEM((3, SIDE, 80, 128), i16),
        pltpu.VMEM((SIDE, 64, 128), F32),
        pltpu.VMEM((SIDE, 64, 128), F32),
        pltpu.VMEM((2, SIDE, 64, 128), F32),
        pltpu.VMEM((WIDE, 16, 128), F32),
        pltpu.VMEM((NZ, 16, 128), F32),
        pltpu.VMEM((NZ, 16, 128), F32),
        pltpu.SemaphoreType.REGULAR, pltpu.SemaphoreType.REGULAR, pltpu.SemaphoreType.REGULAR,
        dma((3,)),
        dma((len(CHUNKS), 8)), dma((len(CHUNKS), 8)),
        dma((SIDE,)), dma((SIDE,)),
        dma((4, SIDE)), dma((4, SIDE)),
        dma((3, SIDE)), dma((3, SIDE)),
        dma((2 * SIDE,)), dma((2, SIDE)),
        dma, dma,
    ]
    return pl.pallas_call(
        kernel,
        out_shape=jax.ShapeDtypeStruct((REPLICAS, 32, COLS), F32),
        in_specs=[hbm, hbm, hbm, pl.BlockSpec(memory_space=pltpu.SMEM)],
        out_specs=vmem,
        scratch_shapes=scratch,
        compiler_params=pltpu.CompilerParams(
            collective_id=0, has_side_effects=True, vmem_limit_bytes=62 * 1024 * 1024),
        cost_estimate=pl.CostEstimate(flops=2 * 1024 * 1024 * k_all, bytes_accessed=2 * 1024 * 1024, transcendentals=0),
    )(coded, exponents, boot_counts, tile_rows)


def solution(mesh):
    placed = (P("narrow", "wide"), P("narrow", "wide"), P(None, "wide"), P())
    return jax.shard_map(
        per_device, mesh=mesh, in_specs=placed, out_specs=P(None, "wide", "narrow"), check_vma=False
    )
```

```python
import jax
import jax.numpy as jnp
from jax import lax
from jax.experimental import pallas as pl
from jax.experimental.pallas import tpu as pltpu
from jax.sharding import PartitionSpec as P

MESH = pl.DeviceIdType.MESH
QB = 32
SIDE = 4
NZ = 16
WIDE = 32
COLS = 64
HALF = 32
REPLICAS = 16
TOTAL = 98304
UNIT = 256
CHUNKS = ((0, 5), (5, 5), (10, 2))
F32 = jnp.float32
BF16 = jnp.bfloat16


def remote(src, dst, send_sem, recv_sem, wide, narrow):
    return pltpu.make_async_remote_copy(
        src_ref=src, dst_ref=dst, send_sem=send_sem, recv_sem=recv_sem,
        device_id={"wide": wide, "narrow": narrow}, device_id_type=MESH,
    )


def scale_exponent(largest):
    return jnp.ceil(jnp.log2(jnp.maximum(largest, 1e-30)))


def to_int16(values, factor):
    scaled = jnp.floor(values * factor + 0.5)
    return jnp.clip(scaled, -32767.0, 32767.0).astype(jnp.int32).astype(jnp.int16)


def from_int16(values, factor):
    return values.astype(jnp.int32).astype(F32) * factor


def put_coded(dst, index, parts):
    largest = jnp.max(jnp.abs(parts[0]), axis=0, keepdims=True)
    for part in parts[1:]:
        largest = jnp.maximum(largest, jnp.max(jnp.abs(part), axis=0, keepdims=True))
    exponent = scale_exponent(largest)
    factor = jnp.exp2(15.0 - exponent)
    dst[(*index, pl.ds(0, 16))] = jnp.broadcast_to(exponent, (16, 128)).astype(jnp.int32).astype(jnp.int16)
    row = 16
    for part in parts:
        dst[(*index, pl.ds(row, part.shape[0]))] = to_int16(part, factor)
        row += part.shape[0]


def get_coded(src, index, place=0):
    tile = src[(*index, pl.ds(0, 16))].astype(jnp.int32).astype(F32)
    factor = jnp.exp2(tile[0:1] - 15.0)
    return from_int16(src[(*index, pl.ds(16 + 64 * place, 64))], factor)


def kernel(coded_in, exponents_in, counts_in, tile_rows, out,
           coded, exponents, counts, xl, yl, cb, acc1, acc2, peer1, peer2, u, q1, near, far, u2, q2, last, own, f_buf,
           tiles, swapped, send_tiles, got,
           known1, known2, known4, ins, gs, gr, ps, pr, s1s, s1r, s2s, s2r, x2s, x2r):
    w = lax.axis_index("wide")
    n = lax.axis_index("narrow")
    z, c = w // 2, w % 2
    x, y = n // SIDE, n % SIDE
    units = coded.shape[1] // UNIT

    def at(x_, y_):
        return lax.rem(x_ + SIDE, SIDE) * SIDE + lax.rem(y_ + SIDE, SIDE)

    def zc(z_, c_):
        return lax.rem(z_ + NZ, NZ) * 2 + c_

    inputs = [
        pltpu.make_async_copy(src, dst, ins.at[i])
        for i, (src, dst) in enumerate(((coded_in, coded), (exponents_in, exponents), (counts_in, counts)))
    ]
    barrier = pltpu.get_barrier_semaphore()
    for narrow in (at(x + 1, y), at(x - 1, y), at(x, y + 1), at(x, y - 1)):
        pl.semaphore_signal(barrier, inc=1, device_id={"wide": w, "narrow": narrow}, device_id_type=MESH)
    for wide in (zc(z, 1 - c), zc(z + 1, c), zc(z - 1, c)):
        pl.semaphore_signal(barrier, inc=1, device_id={"wide": wide, "narrow": n}, device_id_type=MESH)

    for copy in inputs:
        copy.start()
    for copy in inputs[:2]:
        copy.wait()
    for k in range(units):
        cols = pl.ds(k * UNIT, UNIT)
        for half in range(2):
            scale = jnp.exp2(exponents[half:half + 1, cols].astype(F32))
            rows = pl.ds(half * QB, QB)
            block = (coded[rows, cols].astype(F32) * scale).astype(BF16)
            xl[k, y, rows, :] = block
            yl[k, x, rows, :] = block

    pl.semaphore_wait(barrier, 7)

    def tell(sem, d):
        for wide in (zc(z + d, c), zc(z - d, c)):
            pl.semaphore_signal(sem, inc=1, device_id={"wide": wide, "narrow": n}, device_id_type=MESH)

    spans = [pl.ds(*chunk) for chunk in CHUNKS]

    def own_copies(kc):
        src = xl.at[spans[kc], y]
        return [
            remote(src, xl.at[spans[kc], y], gs.at[kc, 0], gr.at[kc, 0], w, at(x, y + 1)),
            remote(src, xl.at[spans[kc], y], gs.at[kc, 1], gr.at[kc, 1], w, at(x, y - 1)),
            remote(src, yl.at[spans[kc], x], gs.at[kc, 2], gr.at[kc, 2], w, at(x + 1, y)),
            remote(src, yl.at[spans[kc], x], gs.at[kc, 3], gr.at[kc, 3], w, at(x - 1, y)),
        ]

    def wrap(v):
        return lax.rem(v + SIDE, SIDE)

    lo, hi = pl.ds(0, HALF), pl.ds(HALF, HALF)

    def forward_copies(kc):
        ym, yp, xm, xp = wrap(y - 1), wrap(y + 1), wrap(x - 1), wrap(x + 1)
        return [
            remote(xl.at[spans[kc], ym, lo], xl.at[spans[kc], ym, lo], gs.at[kc, 4], gr.at[kc, 4], w, at(x, y + 1)),
            remote(xl.at[spans[kc], yp, hi], xl.at[spans[kc], yp, hi], gs.at[kc, 5], gr.at[kc, 5], w, at(x, y - 1)),
            remote(yl.at[spans[kc], xm, lo], yl.at[spans[kc], xm, lo], gs.at[kc, 6], gr.at[kc, 6], w, at(x + 1, y)),
            remote(yl.at[spans[kc], xp, hi], yl.at[spans[kc], xp, hi], gs.at[kc, 7], gr.at[kc, 7], w, at(x - 1, y)),
        ]

    def wait_near(kc):
        places = [xl.at[spans[kc], wrap(y - 1)], xl.at[spans[kc], wrap(y + 1)], yl.at[spans[kc], wrap(x - 1)], yl.at[spans[kc], wrap(x + 1)]]
        for i, place in enumerate(places):
            remote(place, place, gs.at[kc, i], gr.at[kc, i], w, at(x, y + 1)).wait_recv()

    def wait_far(kc):
        yo, xo = wrap(y + 2), wrap(x + 2)
        places = [xl.at[spans[kc], yo, lo], xl.at[spans[kc], yo, hi], yl.at[spans[kc], xo, lo], yl.at[spans[kc], xo, hi]]
        for i, place in enumerate(places):
            remote(place, place, gs.at[kc, 4 + i], gr.at[kc, 4 + i], w, at(x, y + 1)).wait_recv()

    dims = (((1,), (1,)), ((), ()))

    def joined(pieces):
        return jnp.concatenate(pieces, axis=1)

    def parts_of(kc):
        start, count = CHUNKS[kc]
        return range(start, start + count)

    def first(kc):
        rows = joined([yl[k].reshape(SIDE * COLS, UNIT) for k in parts_of(kc)])
        feats = [xl[k, :, 0:HALF, :].reshape(8, 16, UNIT) for k in parts_of(kc)]
        for rp in range(REPLICAS // 2):
            cols = [
                joined([(f * cb[k, r][None]).reshape(128, UNIT) for f, k in zip(feats, parts_of(kc))])
                for r in (2 * rp, 2 * rp + 1)
            ]
            res = lax.dot_general(rows, jnp.concatenate(cols, axis=0), dims, preferred_element_type=F32)
            if kc == 0:
                acc1[rp] = res
            else:
                acc1[rp] += res

    def second(kc, x1):
        rows = joined([xl[k].reshape(SIDE * COLS, UNIT) for k in parts_of(kc)])
        cols = []
        for k in parts_of(kc):
            feats = yl[k, x1, HALF:COLS, :].reshape(1, 2, 16, UNIT)
            cols.append((feats * cb[k][:, None]).reshape(HALF * REPLICAS, UNIT))
        res = lax.dot_general(joined(cols), rows, dims, preferred_element_type=F32)
        if kc == 0:
            acc2[x1] = res
        else:
            acc2[x1] += res

    def second_all(kc, then=None):
        for x1 in range(SIDE):
            @pl.when(x1 <= x)
            def _():
                second(kc, x1)
                if then is not None:
                    then(x1)

    other = zc(z, 1 - c)

    def peer_copy(kind, s):
        if kind == 0:
            place = (slice(None), pl.ds(64 * s, 64))
            return remote(acc1.at[place], peer1.at[place], ps.at[s], pr.at[s], other, n)
        return remote(acc2.at[s], peer2.at[s], ps.at[s], pr.at[s], other, n)

    def used(kind, s):
        return (s >= x) if kind == 0 else (s <= x)

    def start_all(copies):
        for copy in copies:
            copy.start()

    start_all(own_copies(0))
    start_all(own_copies(1))
    inputs[2].wait()
    for k in range(units):
        for r in range(REPLICAS):
            row = counts[r:r + 1, k * UNIT:(k + 1) * UNIT].astype(F32)
            cb[k, r] = jnp.broadcast_to(row, (16, UNIT)).astype(BF16)
    wait_near(0)
    start_all(forward_copies(0))
    start_all(own_copies(2))
    wait_near(1)
    start_all(forward_copies(1))
    wait_far(0)
    tell(known1, 1)
    first(0)
    wait_near(2)
    start_all(forward_copies(2))
    second_all(0)
    pl.semaphore_wait(known1, 2)
    tell(known2, 2)
    wait_far(1)
    first(1)
    second_all(1)
    wait_far(2)
    pl.semaphore_wait(known2, 2)
    tell(known4, 4)

    @pl.when(c == 1)
    def _():
        first(2)
        for s in range(SIDE):
            @pl.when(used(0, s))
            def _():
                peer_copy(0, s).start()

    def send_second(s):
        @pl.when(c == 0)
        def _():
            peer_copy(1, s).start()

    second_all(2, send_second)

    @pl.when(c == 0)
    def _():
        first(2)

    for kind in range(2):
        for s in range(SIDE):
            @pl.when(jnp.logical_and(c == kind, used(kind, s)))
            def _():
                peer_copy(kind, s).wait_recv()
                for r in range(REPLICAS):
                    if kind == 0:
                        place = (r // 2, pl.ds(64 * s, 64), pl.ds(128 * (r % 2), 128))
                        u[s, r % 4, r // 4] = acc1[place] + peer1[place]
                    else:
                        for half in range(2):
                            place = (s, pl.ds(HALF * r, HALF), pl.ds(128 * half, 128))
                            u[s, r % 4, r // 4, 32 * half:32 * half + 32, :] = acc2[place] + peer2[place]

    def live(s):
        return jnp.logical_or(jnp.logical_and(c == 0, s >= x), jnp.logical_and(c == 1, s <= x))

    cls = lax.rem(z, 4)

    def klass(d):
        return lax.rem(cls + d + 4, 4)

    def near_copies(s):
        return [
            remote(q1.at[s, klass(1)], near.at[0, s], s1s.at[0, s], s1r.at[0, s], zc(z + 1, c), n),
            remote(q1.at[s, klass(-1)], near.at[1, s], s1s.at[1, s], s1r.at[1, s], zc(z - 1, c), n),
            remote(q1.at[s, klass(2), 0], far.at[0, s], s1s.at[2, s], s1r.at[2, s], zc(z + 2, c), n),
            remote(q1.at[s, klass(2), 1], far.at[1, s], s1s.at[3, s], s1r.at[3, s], zc(z - 2, c), n),
        ]

    for s in range(SIDE):
        @pl.when(live(s))
        def _():
            copies = near_copies(s)
            for d, parts in ((2, copies[2:]), (1, copies[:1]), (-1, copies[1:2])):
                for half in range(2):
                    put_coded(q1, (s, klass(d), half), [u[s, klass(d), 2 * half], u[s, klass(d), 2 * half + 1]])
                for copy in parts:
                    copy.start()

    step = z // 4
    place = jnp.where(c == 0, y, x)

    def hop_copy(to, d, rows):
        i = lax.rem(step + d, 4)
        narrow = jnp.where(c == 0, at(x, to), at(to, y))
        return remote(q2.at[to, i, pl.ds(0, rows)], last.at[d, place, pl.ds(0, rows)],
                      s2s.at[d, to], s2r.at[d, place], zc(cls + 4 * i, c), narrow)

    def hop_arrival(src, d, rows):
        spot = last.at[d, src, pl.ds(0, rows)]
        return remote(spot, spot, s2s.at[d, src], s2r.at[d, src], other, n)

    def sized(run):
        for k in range(SIDE):
            pl.when(x == k)(lambda: run(16 + 16 * (SIDE - k)))

    def reduced(s):
        for copy in near_copies(s):
            copy.wait_recv()
        for half in range(2):
            for p in range(2):
                i = 2 * half + p
                u2[s, i] = (
                    (u[s, cls, i] + get_coded(near, (0, s, half), p))
                    + (get_coded(near, (1, s, half), p) + get_coded(far, (half, s), p))
                )

    def repacked(i, to):
        parts = []
        for x1 in reversed(range(SIDE)):
            rows = [u2[x1, i, 8 * k:8 * k + 8, HALF * to:HALF * to + HALF] for k in range(8)]
            parts.append(jnp.concatenate([joined(rows[:4]), joined(rows[4:])], axis=0))
        return parts

    @pl.when(c == 0)
    def _():
        for s in range(SIDE):
            pl.when(s >= x)(lambda: reduced(s))

            @pl.when(s < x)
            def _():
                u2[s] = jnp.zeros((4, 64, 128), F32)

        pl.semaphore_wait(known4, 2)
        for d in (2, 1, 3, 0):
            i = lax.rem(step + d, 4)
            for to in range(SIDE):
                parts = repacked(i, to)

                def ship():
                    put_coded(q2, (to, i), parts)
                    sized(lambda rows: hop_copy(to, d, rows).start())

                if d:
                    ship()
                else:
                    pl.when(to != y)(ship)

                    @pl.when(to == y)
                    def _():
                        own[...] = jnp.concatenate(parts, axis=0)
        for src in range(SIDE):
            for d in (0, 1, 3, 2):
                def arrive():
                    sized(lambda rows: hop_arrival(src, d, rows).wait_recv())
                if d:
                    arrive()
                else:
                    pl.when(src != y)(arrive)
            total = jnp.where(src == y, own[...], get_coded(last, (0, src)))
            for d in (1, 3, 2):
                total = total + get_coded(last, (d, src))
            f_buf[src] = total

    @pl.when(c == 1)
    def _():
        pl.semaphore_wait(known4, 2)
        for s in range(SIDE):
            @pl.when(s <= x)
            def _():
                reduced(s)
                for d in (2, 1, 3, 0):
                    i = lax.rem(step + d, 4)

                    def ship():
                        put_coded(q2, (s, i), [u2[s, i]])
                        hop_copy(s, d, 80).start()

                    if d:
                        ship()
                    else:
                        pl.when(s != x)(ship)

                        @pl.when(s == x)
                        def _():
                            own[...] = u2[s, i]
        for src in range(SIDE):
            @pl.when(src >= x)
            def _():
                for d in (0, 1, 3, 2):
                    if d:
                        hop_arrival(src, d, 80).wait_recv()
                    else:
                        pl.when(src != x)(lambda: hop_arrival(src, d, 80).wait_recv())
                total = jnp.where(src == x, own[...], get_coded(last, (0, src)))
                for d in (1, 3, 2):
                    total = total + get_coded(last, (d, src))
                f_buf[src] = total

            @pl.when(src < x)
            def _():
                f_buf[src] = jnp.zeros((64, 128), F32)

    sub = lax.broadcasted_iota(jnp.int32, (8, 128), 0)
    lane = lax.broadcasted_iota(jnp.int32, (8, 128), 1)
    offset = sub + 8 * (lane // HALF) - lane % HALF - COLS * n - HALF * c

    def put_tile(t, tile):
        tiles[t] = jnp.where(offset + 32 * t >= 0, tile / TOTAL, 0.0)

    @pl.when(c == 0)
    def _():
        for x1 in range(SIDE):
            for y1 in range(SIDE):
                for hh in range(2):
                    put_tile(2 * (SIDE * x1 + y1) + hh, f_buf[y1, pl.ds(16 * (SIDE - 1 - x1) + 8 * hh, 8), :])

    @pl.when(c == 1)
    def _():
        for x1 in range(SIDE):
            for half in range(2):
                turned = f_buf[x1, HALF * half:HALF * half + HALF, :].T
                for k in range(4):
                    rows = [turned[32 * k + 8 * g:32 * k + 8 * g + 8] for g in range(4)]
                    put_tile(2 * SIDE * x1 + 4 * half + k, joined(rows))

    mine = pl.ds(pl.multiple_of(8 * c, 8), 8)
    swap = remote(swapped, send_tiles.at[:, mine], ps.at[SIDE], pr.at[SIDE], other, n)
    for to in range(NZ):
        swapped[to] = tiles[tile_rows[2 * to + 1 - c]]
    swap.start()
    for to in range(NZ):
        send_tiles[to, mine, :] = tiles[tile_rows[2 * to + c]]
    swap.wait_recv()

    def tile_copy(d):
        to = lax.rem(z + d, NZ)
        return remote(send_tiles.at[to], got.at[z], x2s, x2r, zc(to, c), n)

    for d in (8, 7, 9, 6, 10, 5, 11, 4, 12, 3, 13, 2, 14, 1, 15):
        to = lax.rem(z + d, NZ)
        tile_copy(d).start()
    got[z] = send_tiles[z]

    for kc in range(len(CHUNKS)):
        for copy in own_copies(kc) + forward_copies(kc):
            copy.wait_send()
    for kind in range(2):
        for s in range(SIDE):
            @pl.when(jnp.logical_and(c == 1 - kind, used(kind, s)))
            def _():
                peer_copy(kind, s).wait_send()
    for s in range(SIDE):
        @pl.when(live(s))
        def _():
            for copy in near_copies(s):
                copy.wait_send()
    for to in range(SIDE):
        for d in range(4):
            away = jnp.logical_or(d > 0, to != place)

            @pl.when(jnp.logical_and(c == 0, away))
            def _():
                sized(lambda rows: hop_copy(to, d, rows).wait_send())

            @pl.when(jnp.logical_and(jnp.logical_and(c == 1, to <= x), away))
            def _():
                hop_copy(to, d, 80).wait_send()
    swap.wait_send()

    most = pl.ds(0, NZ - 1)
    every = remote(send_tiles.at[most], got.at[most], x2s, x2r, other, n)
    every.wait_recv()
    for r in range(REPLICAS):
        for k in range(4):
            out[r, 8 * k:8 * k + 8, :] = jnp.concatenate(
                [got[r, 8 * kind:8 * kind + 8, HALF * k:HALF * k + HALF] for kind in range(2)], axis=1)
    every.wait_send()


def per_device(coded, exponents, boot_counts, tile_rows):
    k_all = coded.shape[1]
    units = k_all // UNIT
    vmem, hbm = pl.BlockSpec(memory_space=pltpu.VMEM), pl.BlockSpec(memory_space=pltpu.HBM)
    dma = pltpu.SemaphoreType.DMA
    i16 = jnp.int16
    scratch = [
        pltpu.VMEM(coded.shape, BF16),
        pltpu.VMEM(exponents.shape, jnp.int32),
        pltpu.VMEM(boot_counts.shape, jnp.int32),
        pltpu.VMEM((units, SIDE, COLS, UNIT), BF16),
        pltpu.VMEM((units, SIDE, COLS, UNIT), BF16),
        pltpu.VMEM((units, REPLICAS, 16, UNIT), BF16),
        pltpu.VMEM((REPLICAS // 2, 256, 256), F32),
        pltpu.VMEM((SIDE, HALF * REPLICAS, 256), F32),
        pltpu.VMEM((REPLICAS // 2, 256, 256), F32),
        pltpu.VMEM((SIDE, HALF * REPLICAS, 256), F32),
        pltpu.VMEM((SIDE, 4, 4, 64, 128), F32),
        pltpu.VMEM((SIDE, 4, 2, 144, 128), i16),
        pltpu.VMEM((2, SIDE, 2, 144, 128), i16),
        pltpu.VMEM((2, SIDE, 144, 128), i16),
        pltpu.VMEM((SIDE, 4, 64, 128), F32),
        pltpu.VMEM((SIDE, 4, 80, 128), i16),
        pltpu.VMEM((4, SIDE, 80, 128), i16),
        pltpu.VMEM((64, 128), F32),
        pltpu.VMEM((SIDE, 64, 128), F32),
        pltpu.VMEM((WIDE, 8, 128), F32),
        pltpu.VMEM((NZ, 8, 128), F32),
        pltpu.VMEM((NZ, 16, 128), F32),
        pltpu.VMEM((NZ, 16, 128), F32),
        pltpu.SemaphoreType.REGULAR, pltpu.SemaphoreType.REGULAR, pltpu.SemaphoreType.REGULAR,
        dma((3,)),
        dma((len(CHUNKS), 8)), dma((len(CHUNKS), 8)),
        dma((SIDE + 1,)), dma((SIDE + 1,)),
        dma((4, SIDE)), dma((4, SIDE)),
        dma((4, SIDE)), dma((4, SIDE)),
        dma, dma,
    ]
    return pl.pallas_call(
        kernel,
        out_shape=jax.ShapeDtypeStruct((REPLICAS, 32, COLS), F32),
        in_specs=[hbm, hbm, hbm, pl.BlockSpec(memory_space=pltpu.SMEM)],
        out_specs=vmem,
        scratch_shapes=scratch,
        compiler_params=pltpu.CompilerParams(
            collective_id=0, has_side_effects=True, vmem_limit_bytes=62 * 1024 * 1024),
        cost_estimate=pl.CostEstimate(flops=2 * 1024 * 1024 * k_all, bytes_accessed=2 * 1024 * 1024, transcendentals=0),
    )(coded, exponents, boot_counts, tile_rows)


def solution(mesh):
    placed = (P("narrow", "wide"), P("narrow", "wide"), P(None, "wide"), P())
    return jax.shard_map(
        per_device, mesh=mesh, in_specs=placed, out_specs=P(None, "wide", "narrow"), check_vma=False
    )
```

```python
import jax
import jax.numpy as jnp
from jax import lax
from jax.experimental import pallas as pl
from jax.experimental.pallas import tpu as pltpu
from jax.sharding import PartitionSpec as P

MESH = pl.DeviceIdType.MESH
QB = 32
SIDE = 4
NZ = 16
WIDE = 32
COLS = 64
HALF = 32
REPLICAS = 16
HOPS = (6, -6, 2, -2)
TOTAL = 98304
UNIT = 256
CHUNKS = ((0, 5), (5, 5), (10, 2))
F32 = jnp.float32
BF16 = jnp.bfloat16


def remote(src, dst, send_sem, recv_sem, wide, narrow):
    return pltpu.make_async_remote_copy(
        src_ref=src, dst_ref=dst, send_sem=send_sem, recv_sem=recv_sem,
        device_id={"wide": wide, "narrow": narrow}, device_id_type=MESH,
    )


def scale_exponent(largest):
    return jnp.ceil(jnp.log2(jnp.maximum(largest, 1e-30)))


def to_int16(values, factor):
    scaled = jnp.floor(values * factor + 0.5)
    return jnp.clip(scaled, -32767.0, 32767.0).astype(jnp.int32).astype(jnp.int16)


def from_int16(values, factor):
    return values.astype(jnp.int32).astype(F32) * factor


def put_coded(dst, index, parts):
    largest = jnp.max(jnp.abs(parts[0]), axis=0, keepdims=True)
    for part in parts[1:]:
        largest = jnp.maximum(largest, jnp.max(jnp.abs(part), axis=0, keepdims=True))
    exponent = scale_exponent(largest)
    factor = jnp.exp2(15.0 - exponent)
    dst[(*index, pl.ds(0, 16))] = jnp.broadcast_to(exponent, (16, 128)).astype(jnp.int32).astype(jnp.int16)
    row = 16
    for part in parts:
        dst[(*index, pl.ds(row, part.shape[0]))] = to_int16(part, factor)
        row += part.shape[0]


def get_coded(src, index, place=0):
    tile = src[(*index, pl.ds(0, 16))].astype(jnp.int32).astype(F32)
    factor = jnp.exp2(tile[0:1] - 15.0)
    return from_int16(src[(*index, pl.ds(16 + 64 * place, 64))], factor)


def kernel(coded_in, exponents_in, counts_in, tile_rows, out,
           coded, exponents, counts, xl, yl, cb, acc1, acc2, peer1, peer2, u, q1, near, far, u2, q2, last, f_buf,
           tiles, swapped, send_tiles, got,
           known1, known2, known4, ins, gs, gr, ps, pr, s1s, s1r, s2s, s2r, x2s, x2r):
    w = lax.axis_index("wide")
    n = lax.axis_index("narrow")
    z, c = w // 2, w % 2
    x, y = n // SIDE, n % SIDE
    units = coded.shape[1] // UNIT

    def at(x_, y_):
        return lax.rem(x_ + SIDE, SIDE) * SIDE + lax.rem(y_ + SIDE, SIDE)

    def zc(z_, c_):
        return lax.rem(z_ + NZ, NZ) * 2 + c_

    inputs = [
        pltpu.make_async_copy(src, dst, ins.at[i])
        for i, (src, dst) in enumerate(((coded_in, coded), (exponents_in, exponents), (counts_in, counts)))
    ]
    barrier = pltpu.get_barrier_semaphore()
    for narrow in (at(x + 1, y), at(x - 1, y), at(x, y + 1), at(x, y - 1)):
        pl.semaphore_signal(barrier, inc=1, device_id={"wide": w, "narrow": narrow}, device_id_type=MESH)
    for wide in (zc(z, 1 - c), zc(z + 1, c), zc(z - 1, c)):
        pl.semaphore_signal(barrier, inc=1, device_id={"wide": wide, "narrow": n}, device_id_type=MESH)

    for copy in inputs:
        copy.start()
    for copy in inputs[:2]:
        copy.wait()
    for k in range(units):
        cols = pl.ds(k * UNIT, UNIT)
        for half in range(2):
            scale = jnp.exp2(exponents[half:half + 1, cols].astype(F32))
            rows = pl.ds(half * QB, QB)
            block = (coded[rows, cols].astype(F32) * scale).astype(BF16)
            xl[k, y, rows, :] = block
            yl[k, x, rows, :] = block

    pl.semaphore_wait(barrier, 7)

    def tell(sem, d):
        for wide in (zc(z + d, c), zc(z - d, c)):
            pl.semaphore_signal(sem, inc=1, device_id={"wide": wide, "narrow": n}, device_id_type=MESH)

    spans = [pl.ds(*chunk) for chunk in CHUNKS]

    def own_copies(kc):
        src = xl.at[spans[kc], y]
        return [
            remote(src, xl.at[spans[kc], y], gs.at[kc, 0], gr.at[kc, 0], w, at(x, y + 1)),
            remote(src, xl.at[spans[kc], y], gs.at[kc, 1], gr.at[kc, 1], w, at(x, y - 1)),
            remote(src, yl.at[spans[kc], x], gs.at[kc, 2], gr.at[kc, 2], w, at(x + 1, y)),
            remote(src, yl.at[spans[kc], x], gs.at[kc, 3], gr.at[kc, 3], w, at(x - 1, y)),
        ]

    def wrap(v):
        return lax.rem(v + SIDE, SIDE)

    lo, hi = pl.ds(0, HALF), pl.ds(HALF, HALF)

    def forward_copies(kc):
        ym, yp, xm, xp = wrap(y - 1), wrap(y + 1), wrap(x - 1), wrap(x + 1)
        return [
            remote(xl.at[spans[kc], ym, lo], xl.at[spans[kc], ym, lo], gs.at[kc, 4], gr.at[kc, 4], w, at(x, y + 1)),
            remote(xl.at[spans[kc], yp, hi], xl.at[spans[kc], yp, hi], gs.at[kc, 5], gr.at[kc, 5], w, at(x, y - 1)),
            remote(yl.at[spans[kc], xm, lo], yl.at[spans[kc], xm, lo], gs.at[kc, 6], gr.at[kc, 6], w, at(x + 1, y)),
            remote(yl.at[spans[kc], xp, hi], yl.at[spans[kc], xp, hi], gs.at[kc, 7], gr.at[kc, 7], w, at(x - 1, y)),
        ]

    def wait_near(kc):
        places = [xl.at[spans[kc], wrap(y - 1)], xl.at[spans[kc], wrap(y + 1)], yl.at[spans[kc], wrap(x - 1)], yl.at[spans[kc], wrap(x + 1)]]
        for i, place in enumerate(places):
            remote(place, place, gs.at[kc, i], gr.at[kc, i], w, at(x, y + 1)).wait_recv()

    def wait_far(kc):
        yo, xo = wrap(y + 2), wrap(x + 2)
        places = [xl.at[spans[kc], yo, lo], xl.at[spans[kc], yo, hi], yl.at[spans[kc], xo, lo], yl.at[spans[kc], xo, hi]]
        for i, place in enumerate(places):
            remote(place, place, gs.at[kc, 4 + i], gr.at[kc, 4 + i], w, at(x, y + 1)).wait_recv()

    dims = (((1,), (1,)), ((), ()))

    def joined(pieces):
        return jnp.concatenate(pieces, axis=1)

    def parts_of(kc):
        start, count = CHUNKS[kc]
        return range(start, start + count)

    def first(kc):
        rows = joined([yl[k].reshape(SIDE * COLS, UNIT) for k in parts_of(kc)])
        feats = [xl[k, :, 0:HALF, :].reshape(8, 16, UNIT) for k in parts_of(kc)]
        for rp in range(REPLICAS // 2):
            cols = [
                joined([(f * cb[k, r][None]).reshape(128, UNIT) for f, k in zip(feats, parts_of(kc))])
                for r in (2 * rp, 2 * rp + 1)
            ]
            res = lax.dot_general(rows, jnp.concatenate(cols, axis=0), dims, preferred_element_type=F32)
            if kc == 0:
                acc1[rp] = res
            else:
                acc1[rp] += res

    def second(kc, x1):
        rows = joined([xl[k].reshape(SIDE * COLS, UNIT) for k in parts_of(kc)])
        cols = []
        for k in parts_of(kc):
            feats = yl[k, x1, HALF:COLS, :].reshape(1, 2, 16, UNIT)
            cols.append((feats * cb[k][:, None]).reshape(HALF * REPLICAS, UNIT))
        res = lax.dot_general(joined(cols), rows, dims, preferred_element_type=F32)
        if kc == 0:
            acc2[x1] = res
        else:
            acc2[x1] += res

    def second_all(kc, then=None):
        for x1 in range(SIDE):
            @pl.when(x1 <= x)
            def _():
                second(kc, x1)
                if then is not None:
                    then(x1)

    other = zc(z, 1 - c)

    def peer_copy(kind, s):
        if kind == 0:
            place = (slice(None), pl.ds(64 * s, 64))
            return remote(acc1.at[place], peer1.at[place], ps.at[s], pr.at[s], other, n)
        return remote(acc2.at[s], peer2.at[s], ps.at[s], pr.at[s], other, n)

    def used(kind, s):
        return (s >= x) if kind == 0 else (s <= x)

    def start_all(copies):
        for copy in copies:
            copy.start()

    start_all(own_copies(0))
    start_all(own_copies(1))
    inputs[2].wait()
    for k in range(units):
        for r in range(REPLICAS):
            row = counts[r:r + 1, k * UNIT:(k + 1) * UNIT].astype(F32)
            cb[k, r] = jnp.broadcast_to(row, (16, UNIT)).astype(BF16)
    wait_near(0)
    start_all(forward_copies(0))
    start_all(own_copies(2))
    wait_near(1)
    start_all(forward_copies(1))
    wait_far(0)
    tell(known1, 1)
    first(0)
    wait_near(2)
    start_all(forward_copies(2))
    second_all(0)
    pl.semaphore_wait(known1, 2)
    tell(known2, 2)
    wait_far(1)
    first(1)
    second_all(1)
    wait_far(2)
    pl.semaphore_wait(known2, 2)
    tell(known4, 4)

    @pl.when(c == 1)
    def _():
        first(2)
        for s in range(SIDE):
            @pl.when(used(0, s))
            def _():
                peer_copy(0, s).start()

    def send_second(s):
        @pl.when(c == 0)
        def _():
            peer_copy(1, s).start()

    second_all(2, send_second)

    @pl.when(c == 0)
    def _():
        first(2)

    for kind in range(2):
        for s in range(SIDE):
            @pl.when(jnp.logical_and(c == kind, used(kind, s)))
            def _():
                peer_copy(kind, s).wait_recv()
                for r in range(REPLICAS):
                    if kind == 0:
                        place = (r // 2, pl.ds(64 * s, 64), pl.ds(128 * (r % 2), 128))
                        u[s, r % 4, r // 4] = acc1[place] + peer1[place]
                    else:
                        for half in range(2):
                            place = (s, pl.ds(HALF * r, HALF), pl.ds(128 * half, 128))
                            u[s, r % 4, r // 4, 32 * half:32 * half + 32, :] = acc2[place] + peer2[place]

    def live(s):
        return jnp.logical_or(jnp.logical_and(c == 0, s >= x), jnp.logical_and(c == 1, s <= x))

    cls = lax.rem(z + 2, 4)

    def klass(d):
        return lax.rem(cls + d + 4, 4)

    def near_copies(s):
        return [
            remote(q1.at[s, klass(1)], near.at[0, s], s1s.at[0, s], s1r.at[0, s], zc(z + 1, c), n),
            remote(q1.at[s, klass(-1)], near.at[1, s], s1s.at[1, s], s1r.at[1, s], zc(z - 1, c), n),
            remote(q1.at[s, klass(2), 0], far.at[0, s], s1s.at[2, s], s1r.at[2, s], zc(z + 2, c), n),
            remote(q1.at[s, klass(2), 1], far.at[1, s], s1s.at[3, s], s1r.at[3, s], zc(z - 2, c), n),
        ]

    for s in range(SIDE):
        @pl.when(live(s))
        def _():
            copies = near_copies(s)
            for d, parts in ((2, copies[2:]), (1, copies[:1]), (-1, copies[1:2])):
                for half in range(2):
                    put_coded(q1, (s, klass(d), half), [u[s, klass(d), 2 * half], u[s, klass(d), 2 * half + 1]])
                for copy in parts:
                    copy.start()

    place = jnp.where(c == 0, y, x)

    def index_of(d):
        return lax.rem(z + HOPS[d] + NZ, NZ) // 4

    def hop_copy(to, d, rows):
        i = index_of(d)
        narrow = jnp.where(c == 0, at(x, to), at(to, y))
        return remote(q2.at[to, i, pl.ds(0, rows)], last.at[d, place, pl.ds(0, rows)],
                      s2s.at[d, to], s2r.at[d, place], zc(z + HOPS[d], c), narrow)

    def hop_arrival(src, d, rows):
        spot = last.at[d, src, pl.ds(0, rows)]
        return remote(spot, spot, s2s.at[d, src], s2r.at[d, src], other, n)

    def sized(short, run):
        for k in range(SIDE):
            pl.when(jnp.logical_and(x == k, jnp.logical_not(short)))(lambda: run(16 + 16 * (SIDE - k)))
            if k < SIDE - 1:
                pl.when(jnp.logical_and(x == k, short))(lambda: run(16 * (SIDE - k)))

    def reduced(s):
        for copy in near_copies(s):
            copy.wait_recv()
        for half in range(2):
            for p in range(2):
                i = 2 * half + p
                u2[s, i] = (
                    (u[s, cls, i] + get_coded(near, (0, s, half), p))
                    + (get_coded(near, (1, s, half), p) + get_coded(far, (half, s), p))
                )

    def gathered(src):
        return (get_coded(last, (0, src)) + get_coded(last, (1, src))) + (get_coded(last, (2, src)) + get_coded(last, (3, src)))

    def repacked(i, to):
        parts = []
        for x1 in reversed(range(SIDE)):
            rows = [u2[x1, i, 8 * k:8 * k + 8, HALF * to:HALF * to + HALF] for k in range(8)]
            parts.append(jnp.concatenate([joined(rows[:4]), joined(rows[4:])], axis=0))
        return parts

    @pl.when(c == 0)
    def _():
        for s in range(SIDE):
            pl.when(s >= x)(lambda: reduced(s))

            @pl.when(s < x)
            def _():
                u2[s] = jnp.zeros((4, 64, 128), F32)

        pl.semaphore_wait(known4, 2)
        for d in range(4):
            for to in range(SIDE):
                put_coded(q2, (to, index_of(d)), repacked(index_of(d), to))
                sized(to > y, lambda rows: hop_copy(to, d, rows).start())
        for src in range(SIDE):
            for d in reversed(range(4)):
                sized(src < y, lambda rows: hop_arrival(src, d, rows).wait_recv())
            f_buf[src] = gathered(src)

    @pl.when(c == 1)
    def _():
        pl.semaphore_wait(known4, 2)
        for s in range(SIDE):
            @pl.when(s <= x)
            def _():
                reduced(s)
                for d in range(4):
                    put_coded(q2, (s, index_of(d)), [u2[s, index_of(d)]])
                    hop_copy(s, d, 80).start()
        for src in range(SIDE):
            @pl.when(src >= x)
            def _():
                for d in reversed(range(4)):
                    hop_arrival(src, d, 80).wait_recv()
                f_buf[src] = gathered(src)

            @pl.when(src < x)
            def _():
                f_buf[src] = jnp.zeros((64, 128), F32)

    sub = lax.broadcasted_iota(jnp.int32, (8, 128), 0)
    lane = lax.broadcasted_iota(jnp.int32, (8, 128), 1)
    offset = sub + 8 * (lane // HALF) - lane % HALF - COLS * n - HALF * c

    def put_tile(t, tile):
        tiles[t] = jnp.where(offset + 32 * t >= 0, tile / TOTAL, 0.0)

    @pl.when(c == 0)
    def _():
        for x1 in range(SIDE):
            for y1 in range(SIDE):
                for hh in range(2):
                    put_tile(2 * (SIDE * x1 + y1) + hh, f_buf[y1, pl.ds(16 * (SIDE - 1 - x1) + 8 * hh, 8), :])

    @pl.when(c == 1)
    def _():
        for x1 in range(SIDE):
            for half in range(2):
                turned = f_buf[x1, HALF * half:HALF * half + HALF, :].T
                for k in range(4):
                    rows = [turned[32 * k + 8 * g:32 * k + 8 * g + 8] for g in range(4)]
                    put_tile(2 * SIDE * x1 + 4 * half + k, joined(rows))

    mine = pl.ds(pl.multiple_of(8 * c, 8), 8)
    swap = remote(swapped, send_tiles.at[:, mine], ps.at[SIDE], pr.at[SIDE], other, n)
    for to in range(NZ):
        swapped[to] = tiles[tile_rows[2 * to + 1 - c]]
    swap.start()
    for to in range(NZ):
        send_tiles[to, mine, :] = tiles[tile_rows[2 * to + c]]
    swap.wait_recv()

    def tile_copy(d):
        to = lax.rem(z + d, NZ)
        return remote(send_tiles.at[to], got.at[z], x2s, x2r, zc(to, c), n)

    for d in (8, 7, 9, 6, 10, 5, 11, 4, 12, 3, 13, 2, 14, 1, 15):
        to = lax.rem(z + d, NZ)
        tile_copy(d).start()
    got[z] = send_tiles[z]

    for kc in range(len(CHUNKS)):
        for copy in own_copies(kc) + forward_copies(kc):
            copy.wait_send()
    for kind in range(2):
        for s in range(SIDE):
            @pl.when(jnp.logical_and(c == 1 - kind, used(kind, s)))
            def _():
                peer_copy(kind, s).wait_send()
    for s in range(SIDE):
        @pl.when(live(s))
        def _():
            for copy in near_copies(s):
                copy.wait_send()
    for to in range(SIDE):
        for d in range(4):
            @pl.when(c == 0)
            def _():
                sized(to > y, lambda rows: hop_copy(to, d, rows).wait_send())

            @pl.when(jnp.logical_and(c == 1, to <= x))
            def _():
                hop_copy(to, d, 80).wait_send()
    swap.wait_send()

    most = pl.ds(0, NZ - 1)
    every = remote(send_tiles.at[most], got.at[most], x2s, x2r, other, n)
    every.wait_recv()
    for r in range(REPLICAS):
        for k in range(4):
            out[r, 8 * k:8 * k + 8, :] = jnp.concatenate(
                [got[r, 8 * kind:8 * kind + 8, HALF * k:HALF * k + HALF] for kind in range(2)], axis=1)
    every.wait_send()


def per_device(coded, exponents, boot_counts, tile_rows):
    k_all = coded.shape[1]
    units = k_all // UNIT
    vmem, hbm = pl.BlockSpec(memory_space=pltpu.VMEM), pl.BlockSpec(memory_space=pltpu.HBM)
    dma = pltpu.SemaphoreType.DMA
    i16 = jnp.int16
    scratch = [
        pltpu.VMEM(coded.shape, BF16),
        pltpu.VMEM(exponents.shape, jnp.int32),
        pltpu.VMEM(boot_counts.shape, jnp.int32),
        pltpu.VMEM((units, SIDE, COLS, UNIT), BF16),
        pltpu.VMEM((units, SIDE, COLS, UNIT), BF16),
        pltpu.VMEM((units, REPLICAS, 16, UNIT), BF16),
        pltpu.VMEM((REPLICAS // 2, 256, 256), F32),
        pltpu.VMEM((SIDE, HALF * REPLICAS, 256), F32),
        pltpu.VMEM((REPLICAS // 2, 256, 256), F32),
        pltpu.VMEM((SIDE, HALF * REPLICAS, 256), F32),
        pltpu.VMEM((SIDE, 4, 4, 64, 128), F32),
        pltpu.VMEM((SIDE, 4, 2, 144, 128), i16),
        pltpu.VMEM((2, SIDE, 2, 144, 128), i16),
        pltpu.VMEM((2, SIDE, 144, 128), i16),
        pltpu.VMEM((SIDE, 4, 64, 128), F32),
        pltpu.VMEM((SIDE, 4, 80, 128), i16),
        pltpu.VMEM((4, SIDE, 80, 128), i16),
        pltpu.VMEM((SIDE, 64, 128), F32),
        pltpu.VMEM((WIDE, 8, 128), F32),
        pltpu.VMEM((NZ, 8, 128), F32),
        pltpu.VMEM((NZ, 16, 128), F32),
        pltpu.VMEM((NZ, 16, 128), F32),
        pltpu.SemaphoreType.REGULAR, pltpu.SemaphoreType.REGULAR, pltpu.SemaphoreType.REGULAR,
        dma((3,)),
        dma((len(CHUNKS), 8)), dma((len(CHUNKS), 8)),
        dma((SIDE + 1,)), dma((SIDE + 1,)),
        dma((4, SIDE)), dma((4, SIDE)),
        dma((4, SIDE)), dma((4, SIDE)),
        dma, dma,
    ]
    return pl.pallas_call(
        kernel,
        out_shape=jax.ShapeDtypeStruct((REPLICAS, 32, COLS), F32),
        in_specs=[hbm, hbm, hbm, pl.BlockSpec(memory_space=pltpu.SMEM)],
        out_specs=vmem,
        scratch_shapes=scratch,
        compiler_params=pltpu.CompilerParams(
            collective_id=0, has_side_effects=True, vmem_limit_bytes=62 * 1024 * 1024),
        cost_estimate=pl.CostEstimate(flops=2 * 1024 * 1024 * k_all, bytes_accessed=2 * 1024 * 1024, transcendentals=0),
    )(coded, exponents, boot_counts, tile_rows)


def solution(mesh):
    placed = (P("narrow", "wide"), P("narrow", "wide"), P(None, "wide"), P())
    return jax.shard_map(
        per_device, mesh=mesh, in_specs=placed, out_specs=P(None, "wide", "narrow"), check_vma=False
    )
```

```python
import jax
import jax.numpy as jnp
from jax import lax
from jax.experimental import pallas as pl
from jax.experimental.pallas import tpu as pltpu
from jax.sharding import PartitionSpec as P

MESH = pl.DeviceIdType.MESH
QB = 32
SIDE = 4
NZ = 16
WIDE = 32
COLS = 64
HALF = 32
REPLICAS = 16
HOPS = (6, -6, 2, -2)
TOTAL = 98304
UNIT = 256
CHUNKS = ((0, 5), (5, 5), (10, 2))
F32 = jnp.float32
BF16 = jnp.bfloat16


def remote(src, dst, send_sem, recv_sem, wide, narrow):
    return pltpu.make_async_remote_copy(
        src_ref=src, dst_ref=dst, send_sem=send_sem, recv_sem=recv_sem,
        device_id={"wide": wide, "narrow": narrow}, device_id_type=MESH,
    )


def scale_exponent(largest):
    return jnp.ceil(jnp.log2(jnp.maximum(largest, 1e-30)))


def to_int16(values, factor):
    scaled = jnp.floor(values * factor + 0.5)
    return jnp.clip(scaled, -32767.0, 32767.0).astype(jnp.int32).astype(jnp.int16)


def from_int16(values, factor):
    return values.astype(jnp.int32).astype(F32) * factor


def put_coded(dst, index, parts):
    largest = jnp.max(jnp.abs(parts[0]), axis=0, keepdims=True)
    for part in parts[1:]:
        largest = jnp.maximum(largest, jnp.max(jnp.abs(part), axis=0, keepdims=True))
    exponent = scale_exponent(largest)
    factor = jnp.exp2(15.0 - exponent)
    dst[(*index, pl.ds(0, 16))] = jnp.broadcast_to(exponent, (16, 128)).astype(jnp.int32).astype(jnp.int16)
    row = 16
    for part in parts:
        dst[(*index, pl.ds(row, part.shape[0]))] = to_int16(part, factor)
        row += part.shape[0]


def get_coded(src, index, place=0):
    tile = src[(*index, pl.ds(0, 16))].astype(jnp.int32).astype(F32)
    factor = jnp.exp2(tile[0:1] - 15.0)
    return from_int16(src[(*index, pl.ds(16 + 64 * place, 64))], factor)


def kernel(coded_in, exponents_in, counts_in, tile_rows, out,
           coded, exponents, counts, xl, yl, cb, acc1, acc2, peer1, peer2, u, q1, near, far, u2, q2, last, f_buf,
           tiles, swapped, send_tiles, got,
           known1, known2, known4, ins, gs, gr, ps, pr, s1s, s1r, s2s, s2r, x2s, x2r):
    w = lax.axis_index("wide")
    n = lax.axis_index("narrow")
    z, c = w // 2, w % 2
    x, y = n // SIDE, n % SIDE
    units = coded.shape[1] // UNIT

    def at(x_, y_):
        return lax.rem(x_ + SIDE, SIDE) * SIDE + lax.rem(y_ + SIDE, SIDE)

    def zc(z_, c_):
        return lax.rem(z_ + NZ, NZ) * 2 + c_

    inputs = [
        pltpu.make_async_copy(src, dst, ins.at[i])
        for i, (src, dst) in enumerate(((coded_in, coded), (exponents_in, exponents), (counts_in, counts)))
    ]
    barrier = pltpu.get_barrier_semaphore()
    for narrow in (at(x + 1, y), at(x - 1, y), at(x, y + 1), at(x, y - 1)):
        pl.semaphore_signal(barrier, inc=1, device_id={"wide": w, "narrow": narrow}, device_id_type=MESH)
    for wide in (zc(z, 1 - c), zc(z + 1, c), zc(z - 1, c)):
        pl.semaphore_signal(barrier, inc=1, device_id={"wide": wide, "narrow": n}, device_id_type=MESH)

    for copy in inputs:
        copy.start()
    for copy in inputs[:2]:
        copy.wait()
    for k in range(units):
        cols = pl.ds(k * UNIT, UNIT)
        for half in range(2):
            scale = jnp.exp2(exponents[half:half + 1, cols].astype(F32))
            rows = pl.ds(half * QB, QB)
            block = (coded[rows, cols].astype(F32) * scale).astype(BF16)
            xl[k, y, rows, :] = block
            yl[k, x, rows, :] = block

    pl.semaphore_wait(barrier, 7)

    def tell(sem, d):
        for wide in (zc(z + d, c), zc(z - d, c)):
            pl.semaphore_signal(sem, inc=1, device_id={"wide": wide, "narrow": n}, device_id_type=MESH)

    spans = [pl.ds(*chunk) for chunk in CHUNKS]

    def own_copies(kc):
        src = xl.at[spans[kc], y]
        return [
            remote(src, xl.at[spans[kc], y], gs.at[kc, 0], gr.at[kc, 0], w, at(x, y + 1)),
            remote(src, xl.at[spans[kc], y], gs.at[kc, 1], gr.at[kc, 1], w, at(x, y - 1)),
            remote(src, yl.at[spans[kc], x], gs.at[kc, 2], gr.at[kc, 2], w, at(x + 1, y)),
            remote(src, yl.at[spans[kc], x], gs.at[kc, 3], gr.at[kc, 3], w, at(x - 1, y)),
        ]

    def wrap(v):
        return lax.rem(v + SIDE, SIDE)

    lo, hi = pl.ds(0, HALF), pl.ds(HALF, HALF)

    def forward_copies(kc):
        ym, yp, xm, xp = wrap(y - 1), wrap(y + 1), wrap(x - 1), wrap(x + 1)
        return [
            remote(xl.at[spans[kc], ym, lo], xl.at[spans[kc], ym, lo], gs.at[kc, 4], gr.at[kc, 4], w, at(x, y + 1)),
            remote(xl.at[spans[kc], yp, hi], xl.at[spans[kc], yp, hi], gs.at[kc, 5], gr.at[kc, 5], w, at(x, y - 1)),
            remote(yl.at[spans[kc], xm, lo], yl.at[spans[kc], xm, lo], gs.at[kc, 6], gr.at[kc, 6], w, at(x + 1, y)),
            remote(yl.at[spans[kc], xp, hi], yl.at[spans[kc], xp, hi], gs.at[kc, 7], gr.at[kc, 7], w, at(x - 1, y)),
        ]

    def wait_near(kc):
        places = [xl.at[spans[kc], wrap(y - 1)], xl.at[spans[kc], wrap(y + 1)], yl.at[spans[kc], wrap(x - 1)], yl.at[spans[kc], wrap(x + 1)]]
        for i, place in enumerate(places):
            remote(place, place, gs.at[kc, i], gr.at[kc, i], w, at(x, y + 1)).wait_recv()

    def wait_far(kc):
        yo, xo = wrap(y + 2), wrap(x + 2)
        places = [xl.at[spans[kc], yo, lo], xl.at[spans[kc], yo, hi], yl.at[spans[kc], xo, lo], yl.at[spans[kc], xo, hi]]
        for i, place in enumerate(places):
            remote(place, place, gs.at[kc, 4 + i], gr.at[kc, 4 + i], w, at(x, y + 1)).wait_recv()

    dims = (((1,), (1,)), ((), ()))

    def joined(pieces):
        return jnp.concatenate(pieces, axis=1)

    def parts_of(kc):
        start, count = CHUNKS[kc]
        return range(start, start + count)

    def first(kc):
        rows = joined([yl[k].reshape(SIDE * COLS, UNIT) for k in parts_of(kc)])
        feats = [xl[k, :, 0:HALF, :].reshape(8, 16, UNIT) for k in parts_of(kc)]
        for rp in range(REPLICAS // 2):
            cols = [
                joined([(f * cb[k, r][None]).reshape(128, UNIT) for f, k in zip(feats, parts_of(kc))])
                for r in (2 * rp, 2 * rp + 1)
            ]
            res = lax.dot_general(rows, jnp.concatenate(cols, axis=0), dims, preferred_element_type=F32)
            if kc == 0:
                acc1[rp] = res
            else:
                acc1[rp] += res

    def second(kc, x1):
        rows = joined([xl[k].reshape(SIDE * COLS, UNIT) for k in parts_of(kc)])
        cols = []
        for k in parts_of(kc):
            feats = yl[k, x1, HALF:COLS, :].reshape(1, 2, 16, UNIT)
            cols.append((feats * cb[k][:, None]).reshape(HALF * REPLICAS, UNIT))
        res = lax.dot_general(joined(cols), rows, dims, preferred_element_type=F32)
        if kc == 0:
            acc2[x1] = res
        else:
            acc2[x1] += res

    def second_all(kc, then=None):
        for x1 in range(SIDE):
            @pl.when(x1 <= x)
            def _():
                second(kc, x1)
                if then is not None:
                    then(x1)

    other = zc(z, 1 - c)

    def peer_copy(kind, s):
        if kind == 0:
            place = (slice(None), pl.ds(64 * s, 64))
            return remote(acc1.at[place], peer1.at[place], ps.at[s], pr.at[s], other, n)
        return remote(acc2.at[s], peer2.at[s], ps.at[s], pr.at[s], other, n)

    def used(kind, s):
        return (s >= x) if kind == 0 else (s <= x)

    def start_all(copies):
        for copy in copies:
            copy.start()

    start_all(own_copies(0))
    start_all(own_copies(1))
    inputs[2].wait()
    for k in range(units):
        for r in range(REPLICAS):
            row = counts[r:r + 1, k * UNIT:(k + 1) * UNIT].astype(F32)
            cb[k, r] = jnp.broadcast_to(row, (16, UNIT)).astype(BF16)
    wait_near(0)
    start_all(forward_copies(0))
    start_all(own_copies(2))
    wait_near(1)
    start_all(forward_copies(1))
    wait_far(0)
    tell(known1, 1)
    first(0)
    wait_near(2)
    start_all(forward_copies(2))
    second_all(0)
    pl.semaphore_wait(known1, 2)
    tell(known2, 2)
    wait_far(1)
    first(1)
    second_all(1)
    wait_far(2)
    pl.semaphore_wait(known2, 2)
    tell(known4, 4)

    @pl.when(c == 1)
    def _():
        first(2)
        for s in range(SIDE):
            @pl.when(used(0, s))
            def _():
                peer_copy(0, s).start()

    def send_second(s):
        @pl.when(c == 0)
        def _():
            peer_copy(1, s).start()

    second_all(2, send_second)

    @pl.when(c == 0)
    def _():
        first(2)

    def live(s):
        return jnp.logical_or(jnp.logical_and(c == 0, s >= x), jnp.logical_and(c == 1, s <= x))

    cls = lax.rem(z + 2, 4)

    def klass(d):
        return lax.rem(cls + d + 4, 4)

    def near_copies(s):
        return [
            remote(q1.at[s, klass(1)], near.at[0, s], s1s.at[0, s], s1r.at[0, s], zc(z + 1, c), n),
            remote(q1.at[s, klass(-1)], near.at[1, s], s1s.at[1, s], s1r.at[1, s], zc(z - 1, c), n),
            remote(q1.at[s, klass(2), 0], far.at[0, s], s1s.at[2, s], s1r.at[2, s], zc(z + 2, c), n),
            remote(q1.at[s, klass(2), 1], far.at[1, s], s1s.at[3, s], s1r.at[3, s], zc(z - 2, c), n),
        ]

    def send_near(s):
        copies = near_copies(s)
        for d, parts in ((2, copies[2:]), (1, copies[:1]), (-1, copies[1:2])):
            for half in range(2):
                put_coded(q1, (s, klass(d), half), [u[s, klass(d), 2 * half], u[s, klass(d), 2 * half + 1]])
            start_all(parts)

    for kind in range(2):
        for s in range(SIDE):
            @pl.when(jnp.logical_and(c == kind, used(kind, s)))
            def _():
                peer_copy(kind, s).wait_recv()
                for r in range(REPLICAS):
                    if kind == 0:
                        place = (r // 2, pl.ds(64 * s, 64), pl.ds(128 * (r % 2), 128))
                        u[s, r % 4, r // 4] = acc1[place] + peer1[place]
                    else:
                        for half in range(2):
                            place = (s, pl.ds(HALF * r, HALF), pl.ds(128 * half, 128))
                            u[s, r % 4, r // 4, 32 * half:32 * half + 32, :] = acc2[place] + peer2[place]
                send_near(s)

    place = jnp.where(c == 0, y, x)

    def index_of(d):
        return lax.rem(z + HOPS[d] + NZ, NZ) // 4

    def hop_copy(to, d, rows):
        i = index_of(d)
        narrow = jnp.where(c == 0, at(x, to), at(to, y))
        return remote(q2.at[to, i, pl.ds(0, rows)], last.at[d, place, pl.ds(0, rows)],
                      s2s.at[d, to], s2r.at[d, place], zc(z + HOPS[d], c), narrow)

    def hop_arrival(src, d, rows):
        spot = last.at[d, src, pl.ds(0, rows)]
        return remote(spot, spot, s2s.at[d, src], s2r.at[d, src], other, n)

    def sized(short, run):
        for k in range(SIDE):
            pl.when(jnp.logical_and(x == k, jnp.logical_not(short)))(lambda: run(16 + 16 * (SIDE - k)))
            if k < SIDE - 1:
                pl.when(jnp.logical_and(x == k, short))(lambda: run(16 * (SIDE - k)))

    def reduced(s):
        for copy in near_copies(s):
            copy.wait_recv()
        for half in range(2):
            for p in range(2):
                i = 2 * half + p
                u2[s, i] = (
                    (u[s, cls, i] + get_coded(near, (0, s, half), p))
                    + (get_coded(near, (1, s, half), p) + get_coded(far, (half, s), p))
                )

    def gathered(src):
        return (get_coded(last, (0, src)) + get_coded(last, (1, src))) + (get_coded(last, (2, src)) + get_coded(last, (3, src)))

    def repacked(i, to):
        parts = []
        for x1 in reversed(range(SIDE)):
            rows = [u2[x1, i, 8 * k:8 * k + 8, HALF * to:HALF * to + HALF] for k in range(8)]
            parts.append(jnp.concatenate([joined(rows[:4]), joined(rows[4:])], axis=0))
        return parts

    @pl.when(c == 0)
    def _():
        for s in range(SIDE):
            pl.when(s >= x)(lambda: reduced(s))

            @pl.when(s < x)
            def _():
                u2[s] = jnp.zeros((4, 64, 128), F32)

        pl.semaphore_wait(known4, 2)
        for d in range(4):
            for to in range(SIDE):
                put_coded(q2, (to, index_of(d)), repacked(index_of(d), to))
                sized(to > y, lambda rows: hop_copy(to, d, rows).start())
        for src in range(SIDE):
            for d in reversed(range(4)):
                sized(src < y, lambda rows: hop_arrival(src, d, rows).wait_recv())
            f_buf[src] = gathered(src)

    @pl.when(c == 1)
    def _():
        pl.semaphore_wait(known4, 2)
        for s in range(SIDE):
            @pl.when(s <= x)
            def _():
                reduced(s)
                for d in range(4):
                    put_coded(q2, (s, index_of(d)), [u2[s, index_of(d)]])
                    hop_copy(s, d, 80).start()
        for src in range(SIDE):
            @pl.when(src >= x)
            def _():
                for d in reversed(range(4)):
                    hop_arrival(src, d, 80).wait_recv()
                f_buf[src] = gathered(src)

            @pl.when(src < x)
            def _():
                f_buf[src] = jnp.zeros((64, 128), F32)

    sub = lax.broadcasted_iota(jnp.int32, (8, 128), 0)
    lane = lax.broadcasted_iota(jnp.int32, (8, 128), 1)
    offset = sub + 8 * (lane // HALF) - lane % HALF - COLS * n - HALF * c

    def put_tile(t, tile):
        tiles[t] = jnp.where(offset + 32 * t >= 0, tile / TOTAL, 0.0)

    @pl.when(c == 0)
    def _():
        for x1 in range(SIDE):
            for y1 in range(SIDE):
                for hh in range(2):
                    put_tile(2 * (SIDE * x1 + y1) + hh, f_buf[y1, pl.ds(16 * (SIDE - 1 - x1) + 8 * hh, 8), :])

    @pl.when(c == 1)
    def _():
        for x1 in range(SIDE):
            for half in range(2):
                turned = f_buf[x1, HALF * half:HALF * half + HALF, :].T
                for k in range(4):
                    rows = [turned[32 * k + 8 * g:32 * k + 8 * g + 8] for g in range(4)]
                    put_tile(2 * SIDE * x1 + 4 * half + k, joined(rows))

    mine = pl.ds(pl.multiple_of(8 * c, 8), 8)
    swap = remote(swapped, send_tiles.at[:, mine], ps.at[SIDE], pr.at[SIDE], other, n)
    for to in range(NZ):
        swapped[to] = tiles[tile_rows[2 * to + 1 - c]]
    swap.start()
    for to in range(NZ):
        send_tiles[to, mine, :] = tiles[tile_rows[2 * to + c]]
    swap.wait_recv()

    def tile_copy(d):
        to = lax.rem(z + d, NZ)
        return remote(send_tiles.at[to], got.at[z], x2s, x2r, zc(to, c), n)

    for d in (8, 7, 9, 6, 10, 5, 11, 4, 12, 3, 13, 2, 14, 1, 15):
        to = lax.rem(z + d, NZ)
        tile_copy(d).start()
    got[z] = send_tiles[z]

    for kc in range(len(CHUNKS)):
        for copy in own_copies(kc) + forward_copies(kc):
            copy.wait_send()
    for kind in range(2):
        for s in range(SIDE):
            @pl.when(jnp.logical_and(c == 1 - kind, used(kind, s)))
            def _():
                peer_copy(kind, s).wait_send()
    for s in range(SIDE):
        @pl.when(live(s))
        def _():
            for copy in near_copies(s):
                copy.wait_send()
    for to in range(SIDE):
        for d in range(4):
            @pl.when(c == 0)
            def _():
                sized(to > y, lambda rows: hop_copy(to, d, rows).wait_send())

            @pl.when(jnp.logical_and(c == 1, to <= x))
            def _():
                hop_copy(to, d, 80).wait_send()
    swap.wait_send()

    most = pl.ds(0, NZ - 1)
    every = remote(send_tiles.at[most], got.at[most], x2s, x2r, other, n)
    every.wait_recv()
    for r in range(REPLICAS):
        for k in range(4):
            out[r, 8 * k:8 * k + 8, :] = jnp.concatenate(
                [got[r, 8 * kind:8 * kind + 8, HALF * k:HALF * k + HALF] for kind in range(2)], axis=1)
    every.wait_send()


def per_device(coded, exponents, boot_counts, tile_rows):
    k_all = coded.shape[1]
    units = k_all // UNIT
    vmem, hbm = pl.BlockSpec(memory_space=pltpu.VMEM), pl.BlockSpec(memory_space=pltpu.HBM)
    dma = pltpu.SemaphoreType.DMA
    i16 = jnp.int16
    scratch = [
        pltpu.VMEM(coded.shape, BF16),
        pltpu.VMEM(exponents.shape, jnp.int32),
        pltpu.VMEM(boot_counts.shape, jnp.int32),
        pltpu.VMEM((units, SIDE, COLS, UNIT), BF16),
        pltpu.VMEM((units, SIDE, COLS, UNIT), BF16),
        pltpu.VMEM((units, REPLICAS, 16, UNIT), BF16),
        pltpu.VMEM((REPLICAS // 2, 256, 256), F32),
        pltpu.VMEM((SIDE, HALF * REPLICAS, 256), F32),
        pltpu.VMEM((REPLICAS // 2, 256, 256), F32),
        pltpu.VMEM((SIDE, HALF * REPLICAS, 256), F32),
        pltpu.VMEM((SIDE, 4, 4, 64, 128), F32),
        pltpu.VMEM((SIDE, 4, 2, 144, 128), i16),
        pltpu.VMEM((2, SIDE, 2, 144, 128), i16),
        pltpu.VMEM((2, SIDE, 144, 128), i16),
        pltpu.VMEM((SIDE, 4, 64, 128), F32),
        pltpu.VMEM((SIDE, 4, 80, 128), i16),
        pltpu.VMEM((4, SIDE, 80, 128), i16),
        pltpu.VMEM((SIDE, 64, 128), F32),
        pltpu.VMEM((WIDE, 8, 128), F32),
        pltpu.VMEM((NZ, 8, 128), F32),
        pltpu.VMEM((NZ, 16, 128), F32),
        pltpu.VMEM((NZ, 16, 128), F32),
        pltpu.SemaphoreType.REGULAR, pltpu.SemaphoreType.REGULAR, pltpu.SemaphoreType.REGULAR,
        dma((3,)),
        dma((len(CHUNKS), 8)), dma((len(CHUNKS), 8)),
        dma((SIDE + 1,)), dma((SIDE + 1,)),
        dma((4, SIDE)), dma((4, SIDE)),
        dma((4, SIDE)), dma((4, SIDE)),
        dma, dma,
    ]
    return pl.pallas_call(
        kernel,
        out_shape=jax.ShapeDtypeStruct((REPLICAS, 32, COLS), F32),
        in_specs=[hbm, hbm, hbm, pl.BlockSpec(memory_space=pltpu.SMEM)],
        out_specs=vmem,
        scratch_shapes=scratch,
        compiler_params=pltpu.CompilerParams(
            collective_id=0, has_side_effects=True, vmem_limit_bytes=62 * 1024 * 1024),
        cost_estimate=pl.CostEstimate(flops=2 * 1024 * 1024 * k_all, bytes_accessed=2 * 1024 * 1024, transcendentals=0),
    )(coded, exponents, boot_counts, tile_rows)


def solution(mesh):
    placed = (P("narrow", "wide"), P("narrow", "wide"), P(None, "wide"), P())
    return jax.shard_map(
        per_device, mesh=mesh, in_specs=placed, out_specs=P(None, "wide", "narrow"), check_vma=False
    )
```
